128 devices in a mesh: grp: 2 (over core), seq: 8 (over y_hi, z), dp: 8 (over x, y_lo).
Axes of the slice: x: 4, y: 4 (y_hi: 2, y_lo: 2; y = y_hi * 2 + y_lo), z: 4, core: 2. Of those that a mesh axis runs over, the one named last changes fastest.
Arguments:
- features: bfloat16 [8, 2, 8, 32, 16, 512], P('dp', None, None, ('grp', 'seq')), may hold values from -48 to 48
- group_gain: float32 [512], replicated, may hold values from 0.5 to 2
- group_bias: float32 [512], replicated, may hold values from -3 to 3
- conv_weight: bfloat16 [512, 432], replicated, may hold values from -0.0546875 to 0.0546875
- hidden: bfloat16 [2, 1, 8, 1024, 1920], P('grp', None, 'dp', 'seq'), may hold values from -36 to 36
- modulation: float32 [2, 1, 8, 3, 1920], P('grp', None, 'dp'), may hold values from -4 to 4
- timesteps: int32 [2, 1, 8], P('grp', None, 'dp'), may hold values from 0 to 999
- fresh_noise: float32 [2, 1, 8, 1024, 64], P('grp', None, 'dp', 'seq'), may hold values from -6 to 6
- input_weight: bfloat16 [1920, 3072], replicated, may hold values from -0.125 to 0.125
- query_gain: float32 [64], replicated, may hold values from 0.5 to 2
- key_gain: float32 [64], replicated, may hold values from 0.5 to 2
- output_weight: bfloat16 [1920, 1024], replicated, may hold values from -0.1875 to 0.1875
- patch_weight: bfloat16 [1920, 64], replicated, may hold values from -0.125 to 0.125
Outputs:
- weight_grad: float32 [1920, 3072], P(('grp', 'seq', 'dp'))
The draws below stay inside these ranges and needn't reach their ends.
All inputs are finite; a program needn't handle non-finite values.
Results may differ from the reference program's by a relative error of at most 0.004.
Values may be sent and summed in bfloat16 or wider, within the bound.
A program may use at most 192 MiB of HBM per device.

```python
import math
import jax
import jax.numpy as jnp
from jax import lax

D = 1920
HD = 64
HEADS = 16
INNER = 1024
C = 512
GROUPS = 32
ZC = 16
PF = 64
TSTEPS = 1000
CL = 1
ROWS_DEV = 2
LW = 16
LF = 8
LH = 32
PH = 16
PW = 8
TOK = 128
S = 1024
N_GRP = 2
N_SEQ = 8
N_DP = 8


def draw_features(key, part):
    key = jax.random.fold_in(key, 11)
    base_key, channel_key, place_key = jax.random.split(key, 3)
    full_shape = (N_DP, N_GRP * CL, LF, LH, LW, C)
    channel_scale = jnp.exp(jax.random.uniform(channel_key, (C,), jnp.float32, math.log(0.3), math.log(3.0)))
    place_scale = jnp.exp(jax.random.uniform(place_key, full_shape[:5] + (1,), jnp.float32, math.log(0.4), math.log(4.0)))
    base = jnp.clip(jax.random.normal(base_key, full_shape, jnp.float32), -4.0, 4.0)
    return (base * channel_scale * place_scale).astype(jnp.bfloat16)


def draw_hidden(key, part):
    key = jax.random.fold_in(key, 23)
    base_key = jax.random.fold_in(key, 0)
    column_key = jax.random.fold_in(key, 1)
    row_key = jax.random.fold_in(key, 2)
    pair_key = jax.random.fold_in(key, 4)
    full_shape = (N_GRP, CL, N_DP, S, D)
    column_scale = jnp.exp(jax.random.uniform(column_key, (D,), jnp.float32, math.log(0.3), math.log(3.0)))
    row_scale = jnp.exp(jax.random.uniform(row_key, full_shape[:4] + (1,), jnp.float32, math.log(0.3), math.log(3.0)))
    block_count = N_GRP * N_SEQ * N_DP
    block_width = D // block_count
    paired = jax.random.randint(pair_key, (N_GRP, CL, N_DP, 1, 1), 0, block_count)
    column_block = jnp.arange(D, dtype=jnp.int32) // block_width
    boost = jnp.where(column_block == paired, 5.0, 1.0).astype(jnp.float32)
    base = jnp.clip(jax.random.normal(base_key, full_shape, jnp.float32), -4.0, 4.0)
    return jnp.clip(base * column_scale * row_scale * boost, -36.0, 36.0).astype(jnp.bfloat16)


def place_ends(drawn, key, low, high):
    spot = [jax.random.randint(jax.random.fold_in(key, axis), (), 0, length) for axis, length in enumerate(drawn.shape)]
    longest = drawn.shape.index(max(drawn.shape))
    beside = spot[:longest] + [(spot[longest] + 1) % drawn.shape[longest]] + spot[longest + 1:]
    return drawn.at[tuple(spot)].set(low).at[tuple(beside)].set(high)


def level_of(stream_key, shape, cuts, smallest, largest):
    level = 1.0
    for dim, shards_of in cuts:
        steps = jax.random.uniform(jax.random.fold_in(jax.random.fold_in(stream_key, 6), dim), (shards_of,), jnp.float32, smallest / len(cuts), largest / len(cuts))
        level = level * jnp.repeat(jnp.exp(steps), shape[dim] // shards_of).reshape((-1,) + (1,) * (len(shape) - 1 - dim))
    return level


def scatter_about(stream_key, shape, deviation, bound, pieces=(), kind=jnp.bfloat16):
    values = jax.random.normal(stream_key, shape, jnp.float32) * deviation
    if len(pieces) > 0:
        values = level_of(stream_key, shape, pieces, -0.22, 0.18) * values
    return jnp.clip(values, min=-bound, max=bound).astype(kind)


def setup_inputs(seed: int = 0) -> dict:
    arg_keys = jax.random.split(jax.random.key(seed), 14)
    return {
        "features": draw_features(jax.random.fold_in(arg_keys[13], 71), 0),
        "group_gain": jnp.clip(jax.random.uniform(arg_keys[1], (C,), jnp.float32, 0.5, 2.0), 0.5, 2.0),
        "group_bias": scatter_about(arg_keys[2], (C,), 1.0, 3.0, (), jnp.float32),
        "conv_weight": scatter_about(arg_keys[3], (C, 27 * ZC), (27 * C) ** -0.5, 0.0546875),
        "hidden": draw_hidden(jax.random.fold_in(arg_keys[13], 71), 0),
        "modulation": scatter_about(arg_keys[5], (N_GRP, CL, N_DP, 3, D), 0.7, 4.0, ((0, 2), (2, 8)), jnp.float32),
        "timesteps": place_ends(jax.random.randint(arg_keys[6], (N_GRP, CL, N_DP), 0, TSTEPS), jax.random.fold_in(arg_keys[6], 1), 0, TSTEPS - 1).astype(jnp.int32),
        "fresh_noise": scatter_about(arg_keys[7], (N_GRP, CL, N_DP, S, PF), 1.0, 6.0, ((0, 2), (2, 8), (3, 8)), jnp.float32),
        "input_weight": scatter_about(arg_keys[8], (D, 3 * INNER), D ** -0.5, 0.125),
        "query_gain": jnp.clip(jax.random.uniform(arg_keys[9], (HD,), jnp.float32, 0.5, 2.0), 0.5, 2.0),
        "key_gain": jnp.clip(jax.random.uniform(arg_keys[10], (HD,), jnp.float32, 0.5, 2.0), 0.5, 2.0),
        "output_weight": scatter_about(arg_keys[11], (D, INNER), INNER ** -0.5, 0.1875),
        "patch_weight": scatter_about(arg_keys[12], (D, PF), D ** -0.5, 0.125),
    }


latent_scale = 1.15258426
group_eps = 1e-06
layer_eps = 1e-05
head_eps = 1e-06

def rounded(values):
    return lax.optimization_barrier(values.astype(jnp.bfloat16)).astype(jnp.float32)

def layer_norm(values, epsilon):
    average = lax.optimization_barrier(jnp.mean(values, axis=-1, keepdims=True))
    centred = values - average
    variance = lax.optimization_barrier(jnp.mean(centred * centred, axis=-1, keepdims=True))
    return centred * lax.rsqrt(variance + epsilon)

def head_norm(projected, head_gain):
    shaped = projected.reshape(projected.shape[:-1] + (HEADS, HD))
    return (layer_norm(shaped, head_eps) * head_gain).reshape(projected.shape)

def causal_conv(activated, conv_weight):
    frame_count = activated.shape[0]
    row_count = activated.shape[1] - 2
    col_count = activated.shape[2]
    padded = jnp.concatenate([activated[:1], activated[:1], activated], axis=0)
    padded = jnp.pad(padded, ((0, 0), (0, 0), (1, 1), (0, 0)))
    tap_terms = jnp.dot(padded.reshape(-1, padded.shape[-1]), conv_weight, preferred_element_type=jnp.float32)
    tap_terms = tap_terms.reshape(padded.shape[:3] + (27, ZC))
    total_sum = jnp.zeros((frame_count, row_count, col_count, ZC), jnp.float32)
    for time_tap in range(3):
        for row_tap in range(3):
            for column_tap in range(3):
                total_sum = total_sum + tap_terms[time_tap:time_tap + frame_count, row_tap:row_tap + row_count, column_tap:column_tap + col_count, (time_tap * 3 + row_tap) * 3 + column_tap]
    return total_sum * latent_scale

def encode_clip(frames, group_gain, group_bias, conv_weight):
    tiles = N_GRP * N_SEQ
    grouped = frames.astype(jnp.float32).reshape(LF, tiles, ROWS_DEV, LW, GROUPS, C // GROUPS)
    average = lax.optimization_barrier(jnp.mean(grouped, axis=(0, 2, 3, 5), keepdims=True))
    centred = grouped - average
    variance = lax.optimization_barrier(jnp.mean(centred * centred, axis=(0, 2, 3, 5), keepdims=True))
    normed = (centred * lax.rsqrt(variance + group_eps)).reshape(LF, LH, LW, C) * group_gain + group_bias
    activated = jax.nn.silu(normed).astype(jnp.bfloat16)
    padded = jnp.pad(activated, ((0, 0), (1, 1), (0, 0), (0, 0)))
    latent = causal_conv(padded, conv_weight)
    patches = latent.reshape(LF, PH, 2, PW, 2, ZC).transpose(0, 1, 3, 2, 4, 5)
    return patches.reshape(S, PF)

def clip_grads(tokens, latent, adjust, step_id, noise_rows, input_weight, query_gain, key_gain, output_weight, patch_weight):
    shift_rows = adjust[0]
    scale_rows = adjust[1]
    gate_rows = adjust[2]
    normed_tokens = (layer_norm(tokens.astype(jnp.float32), layer_eps) * (1.0 + scale_rows) + shift_rows).astype(jnp.bfloat16)
    projected = jnp.dot(normed_tokens, input_weight, preferred_element_type=jnp.float32)
    query_pre = projected[:, :INNER]
    key_pre = projected[:, INNER:2 * INNER]
    query_heads = rounded(head_norm(query_pre, query_gain)).reshape(S, HEADS, HD)
    key_heads = rounded(head_norm(key_pre, key_gain)).reshape(S, HEADS, HD)
    value_heads = rounded(projected[:, 2 * INNER:]).reshape(S, HEADS, HD)
    noise_angle = (step_id.astype(jnp.float32) / TSTEPS + 0.008) / 1.008 * (math.pi / 2)
    target = jnp.cos(noise_angle) * noise_rows - jnp.sin(noise_angle) * latent

    def shard_pass(kv_total, shard_index):
        row_start = (shard_index * TOK).astype(jnp.int32)
        query_rows = lax.dynamic_slice_in_dim(query_heads, row_start, TOK, 0)
        token_rows = lax.dynamic_slice_in_dim(tokens, row_start, TOK, 0)
        target_rows = lax.dynamic_slice_in_dim(target, row_start, TOK, 0)
        scores = jnp.einsum('qhd,khd->hqk', query_rows, key_heads) * 0.125
        exp_scores = jnp.exp(scores)
        total_sum = lax.optimization_barrier(jnp.sum(exp_scores, axis=-1))
        numerator = jnp.einsum('hqk,khd->qhd', rounded(exp_scores), value_heads)
        attended = rounded(numerator / jnp.transpose(total_sum)[:, :, None])
        branch = jnp.dot(attended.reshape(TOK, INNER).astype(jnp.bfloat16), output_weight.T, preferred_element_type=jnp.float32)
        mixed_rows = token_rows.astype(jnp.float32) + gate_rows * branch
        final_rows, final_back = jax.vjp(lambda row_block: layer_norm(row_block, layer_eps), mixed_rows)
        predicted = jnp.dot(final_rows.astype(jnp.bfloat16), patch_weight, preferred_element_type=jnp.float32)
        pred_grad = (2.0 / PF * (predicted - target_rows)).astype(jnp.bfloat16)
        final_grad = jnp.dot(pred_grad, patch_weight.T, preferred_element_type=jnp.float32)
        mixed_grad = final_back(final_grad)[0]
        branch_grad = (gate_rows * mixed_grad).astype(jnp.bfloat16)
        attended_grad = rounded(jnp.dot(branch_grad, output_weight, preferred_element_type=jnp.float32)).reshape(TOK, HEADS, HD)
        delta_rows = lax.optimization_barrier(jnp.sum(attended_grad * attended, axis=-1))
        probability = exp_scores / total_sum[:, :, None]
        value_grad = jnp.einsum('hqk,qhd->khd', rounded(probability), attended_grad)
        prob_grad = jnp.einsum('qhd,khd->hqk', attended_grad, value_heads)
        score_grad = rounded(probability * (prob_grad - jnp.transpose(delta_rows)[:, :, None]))
        query_grad = jnp.einsum('hqk,khd->qhd', score_grad, key_heads) * 0.125
        key_grad = jnp.einsum('hqk,qhd->khd', score_grad, query_rows) * 0.125
        kv_part = rounded(jnp.concatenate([key_grad.reshape(S, INNER), value_grad.reshape(S, INNER)], axis=1))
        return (kv_total + kv_part, query_grad.reshape(TOK, INNER))
    kv_grad, query_parts = lax.scan(shard_pass, jnp.zeros((S, 2 * INNER), jnp.float32), jnp.arange(N_SEQ, dtype=jnp.int32))
    query_grad = query_parts.reshape(S, INNER)
    query_pre_grad = jax.vjp(lambda row_block: head_norm(row_block, query_gain), query_pre)[1](query_grad)[0]
    key_pre_grad = jax.vjp(lambda row_block: head_norm(row_block, key_gain), key_pre)[1](kv_grad[:, :INNER])[0]
    input_grad = jnp.concatenate([query_pre_grad, key_pre_grad, kv_grad[:, INNER:]], axis=1).astype(jnp.bfloat16)
    return jnp.dot(normed_tokens.T, input_grad, preferred_element_type=jnp.float32)

def reference(features, group_gain, group_bias, conv_weight, hidden, modulation, timesteps, fresh_noise, input_weight, query_gain, key_gain, output_weight, patch_weight):
    clip_count = N_GRP * CL * N_DP
    ordered = features.reshape((N_DP, N_GRP, CL) + features.shape[2:]).transpose(1, 2, 0, 3, 4, 5, 6)
    ordered = ordered.reshape((clip_count,) + features.shape[2:])
    tokens_all = hidden.reshape(clip_count, S, D)
    adjust_all = modulation.reshape(clip_count, 3, D)
    steps_all = timesteps.reshape(clip_count)
    noise_all = fresh_noise.reshape(clip_count, S, PF)

    def one_clip(grad_total, clip_items):
        frames, tokens, adjust, step_id, noise_rows = clip_items
        latent = encode_clip(frames, group_gain, group_bias, conv_weight)
        term = clip_grads(tokens, latent, adjust, step_id, noise_rows, input_weight, query_gain, key_gain, output_weight, patch_weight)
        return (grad_total + term, None)
    grad_total, unused = lax.scan(one_clip, jnp.zeros((D, 3 * INNER), jnp.float32), (ordered, tokens_all, adjust_all, steps_all, noise_all))
    return grad_total
```

```python
import math

import jax
import jax.numpy as jnp
from jax import lax
from jax.experimental import pallas as pl
from jax.experimental.pallas import tpu as pltpu
from jax.sharding import PartitionSpec as P

F32 = jnp.float32
BF16 = jnp.bfloat16
MESH = pl.DeviceIdType.MESH

NG, NS, ND = 2, 8, 8
D = 1920
INNER = 1024
S = 1024
TOK = 128
W3 = 384
C = 512
HALF = D // NG
PART = HALF // ND
OUT_ROWS = 15
KB = 256
LATENT_SCALE = 1.15258426
GROUP_EPS = 1e-06
LAYER_EPS = 1e-05
HEAD_EPS = 1e-06


def mm(a, b):
    return lax.dot_general(a, b, (((1,), (0,)), ((), ())), preferred_element_type=F32)


def mm_nt(a, b):
    return lax.dot_general(a, b, (((1,), (1,)), ((), ())), preferred_element_type=F32)


def norm_rows(x):
    mu = jnp.mean(x, axis=-1, keepdims=True)
    centred = x - mu
    var = jnp.mean(centred * centred, axis=-1, keepdims=True)
    r = lax.rsqrt(var + LAYER_EPS)
    return centred * r, r


def head_norm_t(x):
    x3 = x.reshape(2, 64, x.shape[1])
    mu = jnp.mean(x3, axis=1, keepdims=True)
    centred = x3 - mu
    var = jnp.mean(centred * centred, axis=1, keepdims=True)
    r = lax.rsqrt(var + HEAD_EPS)
    return (centred * r).reshape(x.shape), r[:, 0, :]


def head_norm_back_t(grad, xhat, r):
    g3 = grad.reshape(2, 64, grad.shape[1])
    x3 = xhat.reshape(2, 64, grad.shape[1])
    mean_g = jnp.mean(g3, axis=1, keepdims=True)
    mean_gx = jnp.mean(g3 * x3, axis=1, keepdims=True)
    return ((g3 - mean_g - x3 * mean_gx) * r[:, None, :]).reshape(grad.shape)


def gain_columns(gain_row):
    both = jnp.concatenate([gain_row, gain_row], axis=1)
    return jnp.broadcast_to(both, (128, 128)).T


def group_mean(v, count):
    lane = lax.broadcasted_iota(jnp.int32, v.shape, 1)
    for step in (1, 2, 4, 8):
        up = pltpu.roll(v, C - step, 1)
        down = pltpu.roll(v, step, 1)
        v = v + jnp.where((lane & step) == 0, up, down)
    return v * (1.0 / count)


def kernel(
    trig,
    ggain,
    gbias,
    mod,
    qgain,
    kgain,
    feat_hbm,
    cw_hbm,
    hid_hbm,
    noise_hbm,
    w_hbm,
    wo_hbm,
    wp_hbm,
    out_ref,
    feat,
    cw,
    hid,
    noise,
    wq,
    wo,
    wp,
    ng,
    nT,
    wqT,
    taps,
    vsend,
    vrecv,
    lat,
    ltok,
    qT,
    kT,
    vT,
    qrow,
    kmask,
    vmask,
    xq,
    xk,
    rq,
    rk,
    eT,
    num,
    attT,
    att_row,
    att_tok,
    big,
    fin,
    rstd,
    tokbf,
    ag_tok,
    ag_head,
    agT,
    dqT,
    dk,
    dv,
    ig,
    wg_send,
    wg_own,
    sib,
    dpr,
    acc,
    fsend,
    frecv,
    ld_sem,
    ag_ss,
    ag_rs,
    lt_ss,
    lt_rs,
    a1_ss,
    a1_rs,
    a2_ss,
    a2_rs,
    sb_ss,
    sb_rs,
    dp_ss,
    dp_rs,
    fn_ss,
    fn_rs,
):
    g = lax.axis_index("grp")
    s = lax.axis_index("seq")
    d = lax.axis_index("dp")
    tile = g * NS + s

    def remote(src, dst, ssem, rsem, dev):
        return pltpu.make_async_remote_copy(
            src_ref=src, dst_ref=dst, send_sem=ssem, recv_sem=rsem, device_id=dev, device_id_type=MESH
        )

    def cols(index, width=128):
        return pl.ds(pl.multiple_of(index * width, width), width)

    loads = [
        pltpu.make_async_copy(hid_hbm, hid, ld_sem.at[0]),
        pltpu.make_async_copy(feat_hbm, feat, ld_sem.at[1]),
        pltpu.make_async_copy(cw_hbm, cw, ld_sem.at[2]),
        pltpu.make_async_copy(w_hbm.at[:, cols(s)], wq.at[:, 0:128], ld_sem.at[3]),
        pltpu.make_async_copy(w_hbm.at[:, cols(s + 8)], wq.at[:, 128:256], ld_sem.at[4]),
        pltpu.make_async_copy(w_hbm.at[:, cols(s + 16)], wq.at[:, 256:384], ld_sem.at[5]),
        pltpu.make_async_copy(noise_hbm, noise, ld_sem.at[6]),
        pltpu.make_async_copy(wo_hbm, wo, ld_sem.at[7]),
        pltpu.make_async_copy(wp_hbm, wp, ld_sem.at[8]),
    ]
    for copy in loads:
        copy.start()

    barrier = pltpu.get_barrier_semaphore()

    def greet(dev):
        pl.semaphore_signal(barrier, inc=1, device_id=dev, device_id_type=MESH)

    @pl.loop(1, 16)
    def _(j):
        t = lax.rem(tile + j, 16)
        greet((t // NS, lax.rem(t, NS), d))

    @pl.loop(1, 8)
    def _(j):
        greet((g, s, lax.rem(d + j, ND)))

    @pl.loop(0, 8)
    def _(j):
        me = jnp.logical_and(s == d, j == d)

        @pl.when(jnp.logical_not(me))
        def _():
            greet((g, d, j))
            greet((g, j, s))

    loads[0].wait()
    shift_row = mod[0:1, :]
    scale_row = 1.0 + mod[1:2, :]

    @pl.loop(0, TOK // 16)
    def _(i):
        rows = pl.ds(pl.multiple_of(i * 16, 16), 16)
        y, _ = norm_rows(hid[rows, :].astype(F32))
        ng[s, rows, :] = (y * scale_row + shift_row).astype(BF16)

    selfs = jnp.where(s == d, 2, 0)
    pl.semaphore_wait(barrier, 15 + 7 + 16 - selfs)

    def gather(j):
        peer = lax.rem(s + j, NS)
        return remote(ng.at[s], ng.at[s], ag_ss.at[j], ag_rs.at[s], (g, peer, d))

    @pl.loop(1, 8)
    def _(j):
        gather(j).start()

    loads[1].wait()
    loads[2].wait()
    row_id = lax.broadcasted_iota(jnp.int32, (432, W3), 0)
    col_id = lax.broadcasted_iota(jnp.int32, (432, W3), 1)
    inner = col_id & 127
    src0 = (col_id >> 7) * 144 + (inner >> 4) * 48 + (inner & 15)
    used = inner < 48
    cw_val = cw[...]
    col_w = lax.broadcasted_iota(jnp.int32, (C, C), 0) & 15
    acts = []
    for clip in range(2):
        x = feat[clip * 256 : clip * 256 + 256, :].astype(F32)
        mean = group_mean(jnp.broadcast_to(jnp.sum(x, axis=0, keepdims=True), (8, C)), 4096.0)[0:1]
        centred = x - mean
        var = group_mean(
            jnp.broadcast_to(jnp.sum(centred * centred, axis=0, keepdims=True), (8, C)), 4096.0
        )[0:1]
        normed = centred * lax.rsqrt(var + GROUP_EPS) * ggain[...] + gbias[...]
        acts.append(normed / (1.0 + jnp.exp(-normed)))
    act = jnp.concatenate(acts, axis=0)
    for e in range(3):
        pick = jnp.where(jnp.logical_and(used, row_id == src0 + e * 16), 1.0, 0.0).astype(BF16)
        we = mm(cw_val, pick).astype(BF16)
        if e == 0:
            ae = jnp.where(col_w == 0, 0.0, pltpu.roll(act, 1, 0))
        elif e == 2:
            ae = jnp.where(col_w == 15, 0.0, pltpu.roll(act, C - 1, 0))
        else:
            ae = act
        term = mm(ae.astype(BF16), we)
        if e == 0:
            taps[...] = term
        else:
            taps[...] += term
    for clip in range(2):
        for frame in range(8):
            total = None
            for a in range(3):
                base = (clip * 8 + max(frame + a - 2, 0)) * 32
                piece = taps[base : base + 32, a * 128 : a * 128 + 128]
                total = piece if total is None else total + piece
            vsend[clip * 8 + frame] = total
    vrecv[tile] = vsend[tile]

    def latent_copy(j):
        t = lax.rem(tile + j, 16)
        return remote(
            vsend.at[t], vrecv.at[tile], lt_ss.at[j], lt_rs.at[tile], (t // NS, lax.rem(t, NS), d)
        )

    @pl.loop(1, 16)
    def _(j):
        latent_copy(j).start()

    loads[3].wait()
    loads[4].wait()
    loads[5].wait()

    @pl.loop(0, 15)
    def _(i):
        wqT[:, cols(i)] = wq[cols(i), :].T

    gq = gain_columns(qgain[...])
    gk = gain_columns(kgain[...])
    low = lax.broadcasted_iota(jnp.int32, (128, 128), 1) < 64

    @pl.loop(0, 8)
    def _(j):
        src = lax.rem(s + 8 - j, NS)

        @pl.when(j > 0)
        def _():
            remote(ng.at[src], ng.at[src], ag_ss.at[j], ag_rs.at[src], (g, src, d)).wait_recv()

        here = cols(src)
        nt = ng[src].T
        nT[:, here] = nt
        pT = mm(wqT[...], nt)
        xhat, r = head_norm_t(pT[0:128])
        xq[:, here] = xhat
        rq[:, here] = r
        val = xhat * gq
        qT[:, here] = val.astype(BF16)
        qrow[here, :] = val.T.astype(BF16)
        xhat, r = head_norm_t(pT[128:256])
        xk[:, here] = xhat
        rk[:, here] = r
        val = xhat * gk
        kT[:, here] = val.astype(BF16)
        row = val.T
        kmask[0, here, :] = jnp.where(low, row, 0.0).astype(BF16)
        kmask[1, here, :] = jnp.where(low, 0.0, row).astype(BF16)
        val = pT[256:384]
        vT[:, here] = val.astype(BF16)
        row = val.T
        vmask[0, here, :] = jnp.where(low, row, 0.0).astype(BF16)
        vmask[1, here, :] = jnp.where(low, 0.0, row).astype(BF16)

    num[...] = jnp.zeros_like(num)

    def forward(c, tots):
        rows = cols(c, KB)
        new = []
        for h in range(2):
            e = jnp.exp(mm(kmask[h, rows, :], qT[...]) * 0.125)
            eT[h, rows, :] = e
            new.append(tots[h] + jnp.sum(e, axis=0, keepdims=True))
            hr = slice(h * 64, h * 64 + 64)
            num[hr, :] += mm(vT[hr, rows], e.astype(BF16))
        return tuple(new)

    zero_row = jnp.zeros((1, S), F32)
    tots = lax.fori_loop(0, S // KB, forward, (zero_row, zero_row))
    for h in range(2):
        hr = slice(h * 64, h * 64 + 64)
        num[hr, :] = num[hr, :] / tots[h]

    @pl.loop(0, 8)
    def _(j):
        here = cols(j)
        val = num[:, here]
        attT[:, here] = val.astype(BF16)
        att_row[here, :] = val.T.astype(BF16)

    def att_copy(j):
        peer = lax.rem(s + j, NS)
        return remote(
            att_row.at[cols(peer), :], att_tok.at[:, cols(s)], a1_ss.at[j], a1_rs.at[s], (g, peer, d)
        )

    @pl.loop(1, 8)
    def _(j):
        att_copy(j).start()

    att_tok[:, cols(s)] = att_row[cols(s), :]

    @pl.loop(1, 16)
    def _(j):
        t = lax.rem(tile + j, 16)
        remote(
            vsend.at[t], vrecv.at[t], lt_ss.at[j], lt_rs.at[t], (t // NS, lax.rem(t, NS), d)
        ).wait_recv()

    x = vrecv[...].reshape(512, 128)
    pad = jnp.zeros((16, 128), F32)
    total = jnp.concatenate([pad, x[:-16]], axis=0) + pltpu.roll(x, 112, 1)
    total = total + jnp.concatenate([pltpu.roll(x, 96, 1)[16:], pad], axis=0)
    lane = lax.broadcasted_iota(jnp.int32, (512, 128), 1)
    lat[...] = jnp.where(lane < 16, total * LATENT_SCALE, 0.0)
    tokens = jnp.zeros((128, 128), F32)
    for jj in range(2):
        half = lat[pl.ds(jj, 256, stride=2), :].reshape(16, 2, 8, 128)
        for ii in range(2):
            piece = half[:, ii].reshape(128, 128)
            place = 16 * (2 * ii + jj)
            tokens = tokens + (pltpu.roll(piece, place, 1) if place else piece)
    ltok[...] = tokens

    for index in (6, 7, 8):
        loads[index].wait()

    @pl.loop(1, 8)
    def _(j):
        src = lax.rem(s + 8 - j, NS)
        remote(
            att_row.at[cols(src), :], att_tok.at[:, cols(src)], a1_ss.at[j], a1_rs.at[src], (g, src, d)
        ).wait_recv()

    big[...] = mm_nt(att_tok[...], wo[...])
    gate_row = mod[2:3, :]

    @pl.loop(0, TOK // 16)
    def _(i):
        rows = pl.ds(pl.multiple_of(i * 16, 16), 16)
        mixed = hid[rows, :].astype(F32) + gate_row * big[rows, :]
        y, r = norm_rows(mixed)
        fin[rows, :] = y
        rstd[rows, :] = jnp.broadcast_to(r, (16, 128))
        tokbf[rows, :] = y.astype(BF16)

    target = trig[0] * noise[...] - trig[1] * ltok[:, 0:64]
    pred_grad = ((2.0 / 64) * (mm(tokbf[...], wp[...]) - target)).astype(BF16)
    big[...] = mm_nt(pred_grad, wp[...])

    @pl.loop(0, TOK // 16)
    def _(i):
        rows = pl.ds(pl.multiple_of(i * 16, 16), 16)
        dy = big[rows, :]
        y = fin[rows, :]
        mean_dy = jnp.mean(dy, axis=-1, keepdims=True)
        mean_dyy = jnp.mean(dy * y, axis=-1, keepdims=True)
        dx = (dy - mean_dy - y * mean_dyy) * rstd[rows, 0:1]
        tokbf[rows, :] = (gate_row * dx).astype(BF16)

    ag_tok[...] = mm(tokbf[...], wo[...]).astype(BF16)

    def ag_copy(j):
        peer = lax.rem(s + j, NS)
        return remote(
            ag_tok.at[:, cols(peer)], ag_head.at[cols(s), :], a2_ss.at[j], a2_rs.at[s], (g, peer, d)
        )

    @pl.loop(1, 8)
    def _(j):
        ag_copy(j).start()

    ag_head[cols(s), :] = ag_tok[:, cols(s)]

    @pl.loop(1, 8)
    def _(j):
        src = lax.rem(s + 8 - j, NS)
        remote(
            ag_tok.at[:, cols(src)], ag_head.at[cols(src), :], a2_ss.at[j], a2_rs.at[src], (g, src, d)
        ).wait_recv()

    @pl.loop(0, 8)
    def _(j):
        here = cols(j)
        val = ag_head[here, :].astype(F32).T
        agT[:, here] = val.astype(BF16)
        num[:, here] = val * attT[:, here].astype(F32)

    deltas = [jnp.sum(num[h * 64 : h * 64 + 64, :], axis=0, keepdims=True) for h in range(2)]
    invs = [1.0 / tots[h] for h in range(2)]
    dqT[...] = jnp.zeros_like(dqT)
    low_k = lax.broadcasted_iota(jnp.int32, (KB, 128), 1) < 64

    @pl.loop(0, S // KB)
    def _(c):
        rows = cols(c, KB)
        dvs = []
        dks = []
        for h in range(2):
            p = eT[h, rows, :] * invs[h]
            dp = mm(vmask[h, rows, :], agT[...])
            ds = (p * (dp - deltas[h])).astype(BF16)
            dvs.append(mm(p.astype(BF16), ag_head[...]))
            dks.append(mm(ds, qrow[...]))
            hr = slice(h * 64, h * 64 + 64)
            dqT[hr, :] += mm(kT[hr, rows], ds)
        dv[rows, :] = jnp.where(low_k, dvs[0], dvs[1])
        dk[rows, :] = jnp.where(low_k, dks[0], dks[1]) * 0.125

    @pl.loop(0, 8)
    def _(j):
        here = cols(j)
        grad = head_norm_back_t(dqT[:, here] * 0.125 * gq, xq[:, here], rq[:, here])
        ig[here, 0:128] = grad.T.astype(BF16)
        grad = head_norm_back_t(dk[here, :].T * gk, xk[:, here], rk[:, here])
        ig[here, 128:256] = grad.T.astype(BF16)
        ig[here, 256:384] = dv[here, :].astype(BF16)

    def sib_copy(i):
        return remote(wg_send.at[i], sib.at[i], sb_ss.at[i], sb_rs.at[i], (1 - g, s, d))

    @pl.loop(0, 4)
    def _(i):
        rows = pl.ds(pl.multiple_of((1 - g) * HALF + i * 240, 16), 240)
        wg_send[i] = mm(nT[rows, :], ig[...])
        sib_copy(i).start()

    @pl.loop(0, 4)
    def _(i):
        rows = pl.ds(pl.multiple_of(g * HALF + i * 240, 16), 240)
        value = mm(nT[rows, :], ig[...])
        wg_own[2 * i] = value[0:PART]
        wg_own[2 * i + 1] = value[PART : 2 * PART]

    def dp_copy(c):
        return remote(wg_own.at[c], dpr.at[d], dp_ss.at[c], dp_rs.at[d], (g, s, c))

    @pl.loop(0, 4)
    def _(j):
        i = lax.rem(d // 2 + 1 + j, 4)
        sib_copy(i).wait_recv()
        for q in range(2):
            c = 2 * i + q
            wg_own[c] += sib[i, q * PART : q * PART + PART, :]

            @pl.when(c != d)
            def _():
                dp_copy(c).start()

    acc[PART:, :] = jnp.zeros((128 - PART, W3), F32)
    acc[0:PART, :] = wg_own[d]

    @pl.loop(1, 8)
    def _(j):
        src = lax.rem(d + 8 - j, ND)
        remote(wg_own.at[src], dpr.at[src], dp_ss.at[src], dp_rs.at[src], (g, s, src)).wait_recv()
        acc[0:PART, :] += dpr[src]

    for j in range(8):
        fsend[j] = acc[j * OUT_ROWS : j * OUT_ROWS + 16, :]

    def fin_copy(j):
        return remote(fsend.at[j], frecv.at[s], fn_ss.at[j], fn_rs.at[s], (g, d, j))

    @pl.loop(0, 8)
    def _(j):
        me = jnp.logical_and(s == d, j == d)

        @pl.when(me)
        def _():
            frecv[s] = fsend[j]

        @pl.when(jnp.logical_not(me))
        def _():
            fin_copy(j).start()

    @pl.loop(0, 8)
    def _(j):
        me = jnp.logical_and(s == d, j == d)

        @pl.when(jnp.logical_not(me))
        def _():
            remote(fsend.at[j], frecv.at[j], fn_ss.at[j], fn_rs.at[j], (g, j, s)).wait_recv()

    for j in range(8):
        for part in range(3):
            out_ref[:, part * INNER + j * 128 : part * INNER + j * 128 + 128] = frecv[
                j, 0:OUT_ROWS, part * 128 : part * 128 + 128
            ]

    @pl.loop(1, 8)
    def _(j):
        gather(j).wait_send()
        att_copy(j).wait_send()
        ag_copy(j).wait_send()

    @pl.loop(1, 16)
    def _(j):
        latent_copy(j).wait_send()

    @pl.loop(0, 4)
    def _(i):
        sib_copy(i).wait_send()

    @pl.loop(0, 8)
    def _(c):
        @pl.when(c != d)
        def _():
            dp_copy(c).wait_send()

        me = jnp.logical_and(s == d, c == d)

        @pl.when(jnp.logical_not(me))
        def _():
            fin_copy(c).wait_send()


def scratch_shapes():
    V = pltpu.VMEM
    dma = pltpu.SemaphoreType.DMA
    return [
        V((512, C), BF16),
        V((C, 432), BF16),
        V((TOK, D), BF16),
        V((TOK, 64), F32),
        V((D, W3), BF16),
        V((D, INNER), BF16),
        V((D, 64), BF16),
        V((NS, TOK, D), BF16),
        V((D, S), BF16),
        V((W3, D), BF16),
        V((512, W3), F32),
        V((16, 32, 128), F32),
        V((16, 32, 128), F32),
        V((512, 128), F32),
        V((TOK, 128), F32),
        V((128, S), BF16),
        V((128, S), BF16),
        V((128, S), BF16),
        V((S, 128), BF16),
        V((2, S, 128), BF16),
        V((2, S, 128), BF16),
        V((128, S), F32),
        V((128, S), F32),
        V((2, S), F32),
        V((2, S), F32),
        V((2, S, S), F32),
        V((128, S), F32),
        V((128, S), BF16),
        V((S, 128), BF16),
        V((TOK, INNER), BF16),
        V((TOK, D), F32),
        V((TOK, D), F32),
        V((TOK, 128), F32),
        V((TOK, D), BF16),
        V((TOK, INNER), BF16),
        V((S, 128), BF16),
        V((128, S), BF16),
        V((128, S), F32),
        V((S, 128), F32),
        V((S, 128), F32),
        V((S, W3), BF16),
        V((4, 240, W3), F32),
        V((8, PART, W3), F32),
        V((4, 240, W3), F32),
        V((8, PART, W3), F32),
        V((128, W3), F32),
        V((8, 16, W3), F32),
        V((8, 16, W3), F32),
        dma((9,)),
        dma((8,)),
        dma((8,)),
        dma((16,)),
        dma((16,)),
        dma((8,)),
        dma((8,)),
        dma((8,)),
        dma((8,)),
        dma((4,)),
        dma((4,)),
        dma((8,)),
        dma((8,)),
        dma((8,)),
        dma((8,)),
    ]


def local(
    features,
    group_gain,
    group_bias,
    conv_weight,
    hidden,
    modulation,
    timesteps,
    fresh_noise,
    input_weight,
    query_gain,
    key_gain,
    output_weight,
    patch_weight,
):
    angle = (timesteps.reshape(1).astype(F32) / 1000 + 0.008) / 1.008 * (math.pi / 2)
    trig = jnp.concatenate([jnp.cos(angle), jnp.sin(angle)])
    vmem = pl.BlockSpec(memory_space=pltpu.VMEM)
    hbm = pl.BlockSpec(memory_space=pl.ANY)
    return pl.pallas_call(
        kernel,
        out_shape=jax.ShapeDtypeStruct((OUT_ROWS, 3 * INNER), F32),
        in_specs=[pl.BlockSpec(memory_space=pltpu.SMEM)] + [vmem] * 5 + [hbm] * 7,
        out_specs=vmem,
        scratch_shapes=scratch_shapes(),
        compiler_params=pltpu.CompilerParams(
            collective_id=0, has_side_effects=True, vmem_limit_bytes=60 * 2**20
        ),
    )(
        trig,
        group_gain.reshape(1, C),
        group_bias.reshape(1, C),
        modulation.reshape(3, D),
        query_gain.reshape(1, 64),
        key_gain.reshape(1, 64),
        features.reshape(512, C),
        conv_weight,
        hidden.reshape(TOK, D),
        fresh_noise.reshape(TOK, 64),
        input_weight,
        output_weight,
        patch_weight,
    )


def solution(mesh):
    in_specs = (
        P("dp", None, None, ("grp", "seq"), None, None),
        P(),
        P(),
        P(),
        P("grp", None, "dp", "seq", None),
        P("grp", None, "dp", None, None),
        P("grp", None, "dp"),
        P("grp", None, "dp", "seq", None),
        P(),
        P(),
        P(),
        P(),
        P(),
    )
    out_specs = P(("grp", "seq", "dp"), None)
    return jax.shard_map(local, mesh=mesh, in_specs=in_specs, out_specs=out_specs, check_vma=False)
```

```python
import math

import jax
import jax.numpy as jnp
from jax import lax
from jax.experimental import pallas as pl
from jax.experimental.pallas import tpu as pltpu
from jax.sharding import PartitionSpec as P

F32 = jnp.float32
BF16 = jnp.bfloat16
MESH = pl.DeviceIdType.MESH

NG, NS, ND = 2, 8, 8
D = 1920
INNER = 1024
S = 1024
TOK = 128
W3 = 384
C = 512
HALF = D // NG
PART = HALF // ND
OUT_ROWS = 15
KB = 256
LATENT_SCALE = 1.15258426
GROUP_EPS = 1e-06
LAYER_EPS = 1e-05
HEAD_EPS = 1e-06


def mm(a, b):
    return lax.dot_general(a, b, (((1,), (0,)), ((), ())), preferred_element_type=F32)


def mm_nt(a, b):
    return lax.dot_general(a, b, (((1,), (1,)), ((), ())), preferred_element_type=F32)


def norm_rows(x):
    mu = jnp.mean(x, axis=-1, keepdims=True)
    centred = x - mu
    var = jnp.mean(centred * centred, axis=-1, keepdims=True)
    r = lax.rsqrt(var + LAYER_EPS)
    return centred * r, r


def head_norm_t(x):
    x3 = x.reshape(2, 64, x.shape[1])
    mu = jnp.mean(x3, axis=1, keepdims=True)
    centred = x3 - mu
    var = jnp.mean(centred * centred, axis=1, keepdims=True)
    r = lax.rsqrt(var + HEAD_EPS)
    return (centred * r).reshape(x.shape), r[:, 0, :]


def head_norm_back_t(grad, xhat, r):
    g3 = grad.reshape(2, 64, grad.shape[1])
    x3 = xhat.reshape(2, 64, grad.shape[1])
    mean_g = jnp.mean(g3, axis=1, keepdims=True)
    mean_gx = jnp.mean(g3 * x3, axis=1, keepdims=True)
    return ((g3 - mean_g - x3 * mean_gx) * r[:, None, :]).reshape(grad.shape)


def gain_columns(gain_row):
    both = jnp.concatenate([gain_row, gain_row], axis=1)
    return jnp.broadcast_to(both, (128, 128)).T


def group_mean(v, count):
    lane = lax.broadcasted_iota(jnp.int32, v.shape, 1)
    for step in (1, 2, 4, 8):
        up = pltpu.roll(v, C - step, 1)
        down = pltpu.roll(v, step, 1)
        v = v + jnp.where((lane & step) == 0, up, down)
    return v * (1.0 / count)


def kernel(
    steps,
    ggain,
    gbias,
    mod,
    qgain,
    kgain,
    feat_hbm,
    cw_hbm,
    hid_hbm,
    noise_hbm,
    w_hbm,
    wo_hbm,
    wp_hbm,
    out_ref,
    feat,
    cw,
    hid,
    noise,
    wq,
    wo,
    wp,
    ng,
    nT,
    wqT,
    taps,
    vsend,
    vrecv,
    lat,
    ltok,
    qT,
    kT,
    vT,
    qrow,
    kmask,
    vmask,
    xq,
    xk,
    rq,
    rk,
    eT,
    num,
    attT,
    att_row,
    att_tok,
    big,
    fin,
    rstd,
    tokbf,
    ag_tok,
    ag_head,
    agT,
    dqT,
    dk,
    dv,
    ig,
    ig_sib,
    nT_sib,
    wg_own,
    dpr,
    acc,
    fsend,
    frecv,
    ld_sem,
    ag_ss,
    ag_rs,
    lt_ss,
    lt_rs,
    a1_ss,
    a1_rs,
    a2_ss,
    a2_rs,
    sb_ss,
    sb_rs,
    dp_ss,
    dp_rs,
    fn_ss,
    fn_rs,
    nt_sem,
):
    g = lax.axis_index("grp")
    s = lax.axis_index("seq")
    d = lax.axis_index("dp")
    tile = g * NS + s

    def remote(src, dst, ssem, rsem, dev):
        return pltpu.make_async_remote_copy(
            src_ref=src, dst_ref=dst, send_sem=ssem, recv_sem=rsem, device_id=dev, device_id_type=MESH
        )

    def cols(index, width=128):
        return pl.ds(pl.multiple_of(index * width, width), width)

    loads = [
        pltpu.make_async_copy(hid_hbm, hid, ld_sem.at[0]),
        pltpu.make_async_copy(feat_hbm, feat, ld_sem.at[1]),
        pltpu.make_async_copy(cw_hbm, cw, ld_sem.at[2]),
        pltpu.make_async_copy(w_hbm.at[:, cols(s)], wq.at[:, 0:128], ld_sem.at[3]),
        pltpu.make_async_copy(w_hbm.at[:, cols(s + 8)], wq.at[:, 128:256], ld_sem.at[4]),
        pltpu.make_async_copy(w_hbm.at[:, cols(s + 16)], wq.at[:, 256:384], ld_sem.at[5]),
        pltpu.make_async_copy(noise_hbm, noise, ld_sem.at[6]),
        pltpu.make_async_copy(wo_hbm, wo, ld_sem.at[7]),
        pltpu.make_async_copy(wp_hbm, wp, ld_sem.at[8]),
    ]
    for copy in loads:
        copy.start()

    barrier = pltpu.get_barrier_semaphore()

    def greet(dev):
        pl.semaphore_signal(barrier, inc=1, device_id=dev, device_id_type=MESH)

    @pl.loop(1, 16)
    def _(j):
        t = lax.rem(tile + j, 16)
        greet((t // NS, lax.rem(t, NS), d))

    @pl.loop(1, 8)
    def _(j):
        greet((g, s, lax.rem(d + j, ND)))

    @pl.loop(0, 8)
    def _(j):
        me = jnp.logical_and(s == d, j == d)

        @pl.when(jnp.logical_not(me))
        def _():
            greet((g, d, j))
            greet((g, j, s))

    loads[0].wait()
    shift_row = mod[0]
    scale_row = 1.0 + mod[1]

    @pl.loop(0, TOK // 16)
    def _(i):
        rows = pl.ds(pl.multiple_of(i * 16, 16), 16)
        y, _ = norm_rows(hid[rows, :].astype(F32))
        ng[s, rows, :] = (y * scale_row + shift_row).astype(BF16)

    selfs = jnp.where(s == d, 2, 0)
    pl.semaphore_wait(barrier, 15 + 7 + 16 - selfs)

    yh, z = s // 4, lax.rem(s, 4)
    z_up = yh * 4 + lax.rem(z + 1, 4)
    z_down = yh * 4 + lax.rem(z + 3, 4)
    across = (1 - yh) * 4 + z

    def pass_on(slot, half, sem, peer):
        block = ng.at[slot, pl.ds(half * 64, 64), :]
        return remote(block, block, ag_ss.at[sem], ag_rs.at[slot * 2 + half], (g, peer, d))

    own_sends = [
        pass_on(s, half, half * 3 + k, peer)
        for half in range(2)
        for k, peer in enumerate((z_up, z_down, across))
    ]
    for copy in own_sends:
        copy.start()

    loads[1].wait()
    loads[2].wait()
    row_id = lax.broadcasted_iota(jnp.int32, (W3, 432), 1)
    col_id = lax.broadcasted_iota(jnp.int32, (W3, 432), 0)
    inner = col_id & 127
    src0 = (col_id >> 7) * 144 + (inner >> 4) * 48 + (inner & 15)
    used = inner < 48
    cw_val = cw[...]
    col_w = lax.broadcasted_iota(jnp.int32, (C, C), 0) & 15
    acts = []
    for clip in range(2):
        x = feat[clip * 256 : clip * 256 + 256, :].astype(F32)
        mean = group_mean(jnp.broadcast_to(jnp.sum(x, axis=0, keepdims=True), (8, C)), 4096.0)[0:1]
        centred = x - mean
        var = group_mean(
            jnp.broadcast_to(jnp.sum(centred * centred, axis=0, keepdims=True), (8, C)), 4096.0
        )[0:1]
        normed = centred * lax.rsqrt(var + GROUP_EPS) * ggain[...] + gbias[...]
        acts.append(normed / (1.0 + jnp.exp(-normed)))
    act = jnp.concatenate(acts, axis=0)
    for e in range(3):
        pick = jnp.where(jnp.logical_and(used, row_id == src0 + e * 16), 1.0, 0.0).astype(BF16)
        we = mm(pick, cw_val).astype(BF16)
        if e == 0:
            ae = jnp.where(col_w == 0, 0.0, pltpu.roll(act, 1, 0))
        elif e == 2:
            ae = jnp.where(col_w == 15, 0.0, pltpu.roll(act, C - 1, 0))
        else:
            ae = act
        term = mm_nt(ae.astype(BF16), we)
        if e == 0:
            taps[...] = term
        else:
            taps[...] += term
    for clip in range(2):
        for frame in range(8):
            total = None
            for a in range(3):
                base = (clip * 8 + max(frame + a - 2, 0)) * 32
                piece = taps[base : base + 32, a * 128 : a * 128 + 128]
                total = piece if total is None else total + piece
            vsend[clip * 8 + frame] = total
    vrecv[tile] = vsend[tile]

    def latent_copy(j):
        t = lax.rem(tile + j, 16)
        return remote(
            vsend.at[t], vrecv.at[tile], lt_ss.at[j], lt_rs.at[tile], (t // NS, lax.rem(t, NS), d)
        )

    @pl.loop(1, 16)
    def _(j):
        latent_copy(j).start()

    loads[3].wait()
    loads[4].wait()
    loads[5].wait()

    @pl.loop(0, 15)
    def _(i):
        wqT[:, cols(i)] = wq[cols(i), :].T

    gq = gain_columns(qgain[...])
    gk = gain_columns(kgain[...])
    low = lax.broadcasted_iota(jnp.int32, (128, 128), 1) < 64

    @pl.loop(0, 8)
    def _(j):
        other = jnp.logical_or(j == 3, j >= 5)
        hop = jnp.where(
            jnp.logical_or(j == 1, j == 5), 3, jnp.where(jnp.logical_or(j == 2, j == 6), 1, 0)
        )
        hop = jnp.where(jnp.logical_or(j == 4, j == 7), 2, hop)
        src = jnp.where(other, 1 - yh, yh) * 4 + lax.rem(z + hop, 4)

        @pl.when(j > 0)
        def _():
            for half in range(2):
                pass_on(src, half, 0, z_up).wait_recv()

                if half == 0:

                    @pl.when(j == 1)
                    def _():
                        pass_on(src, 0, 6, z_up).start()

                else:

                    @pl.when(j == 2)
                    def _():
                        pass_on(src, 1, 7, z_down).start()

                @pl.when(j == 3)
                def _():
                    pass_on(src, half, 8 + 2 * half, z_up).start()
                    pass_on(src, half, 9 + 2 * half, z_down).start()

                @pl.when(j == 4)
                def _():
                    pass_on(src, half, 12 + half, across).start()

        here = cols(src)
        nt = ng[src].T
        nT[:, here] = nt
        pT = mm(wqT[...], nt)
        xhat, r = head_norm_t(pT[0:128])
        xq[:, here] = xhat
        rq[:, here] = r
        val = xhat * gq
        qT[:, here] = val.astype(BF16)
        qrow[here, :] = val.T.astype(BF16)
        xhat, r = head_norm_t(pT[128:256])
        xk[:, here] = xhat
        rk[:, here] = r
        val = xhat * gk
        kT[:, here] = val.astype(BF16)
        row = val.T
        kmask[0, here, :] = jnp.where(low, row, 0.0).astype(BF16)
        kmask[1, here, :] = jnp.where(low, 0.0, row).astype(BF16)
        val = pT[256:384]
        vT[:, here] = val.astype(BF16)
        row = val.T
        vmask[0, here, :] = jnp.where(low, row, 0.0).astype(BF16)
        vmask[1, here, :] = jnp.where(low, 0.0, row).astype(BF16)

    norm_copy = remote(
        nT.at[pl.ds(pl.multiple_of((1 - g) * HALF, 16), HALF), :],
        nT_sib,
        nt_sem.at[0],
        nt_sem.at[1],
        (1 - g, s, d),
    )
    norm_copy.start()

    num[...] = jnp.zeros_like(num)

    def forward(c, tots):
        rows = cols(c, KB)
        new = []
        for h in range(2):
            e = jnp.exp(mm(kmask[h, rows, :], qT[...]) * 0.125)
            eT[h, rows, :] = e
            new.append(tots[h] + jnp.sum(e, axis=0, keepdims=True))
            hr = slice(h * 64, h * 64 + 64)
            num[hr, :] += mm(vT[hr, rows], e.astype(BF16))
        return tuple(new)

    zero_row = jnp.zeros((1, S), F32)
    tots = lax.fori_loop(0, S // KB, forward, (zero_row, zero_row))
    for h in range(2):
        hr = slice(h * 64, h * 64 + 64)
        num[hr, :] = num[hr, :] / tots[h]

    @pl.loop(0, 8)
    def _(j):
        here = cols(j)
        val = num[:, here]
        attT[:, here] = val.astype(BF16)
        att_row[here, :] = val.T.astype(BF16)

    def att_copy(j):
        peer = lax.rem(s + j, NS)
        return remote(
            att_row.at[cols(peer), :], att_tok.at[:, cols(s)], a1_ss.at[j], a1_rs.at[s], (g, peer, d)
        )

    @pl.loop(1, 8)
    def _(j):
        att_copy(j).start()

    att_tok[:, cols(s)] = att_row[cols(s), :]

    @pl.loop(1, 16)
    def _(j):
        t = lax.rem(tile + j, 16)
        remote(
            vsend.at[t], vrecv.at[t], lt_ss.at[j], lt_rs.at[t], (t // NS, lax.rem(t, NS), d)
        ).wait_recv()

    x = vrecv[...].reshape(512, 128)
    pad = jnp.zeros((16, 128), F32)
    total = jnp.concatenate([pad, x[:-16]], axis=0) + pltpu.roll(x, 112, 1)
    total = total + jnp.concatenate([pltpu.roll(x, 96, 1)[16:], pad], axis=0)
    lane = lax.broadcasted_iota(jnp.int32, (512, 128), 1)
    lat[...] = jnp.where(lane < 16, total * LATENT_SCALE, 0.0)
    tokens = jnp.zeros((128, 128), F32)
    for jj in range(2):
        half = lat[pl.ds(jj, 256, stride=2), :].reshape(16, 2, 8, 128)
        for ii in range(2):
            piece = half[:, ii].reshape(128, 128)
            place = 16 * (2 * ii + jj)
            tokens = tokens + (pltpu.roll(piece, place, 1) if place else piece)
    ltok[...] = tokens

    for index in (6, 7, 8):
        loads[index].wait()

    @pl.loop(1, 8)
    def _(j):
        src = lax.rem(s + 8 - j, NS)
        remote(
            att_row.at[cols(src), :], att_tok.at[:, cols(src)], a1_ss.at[j], a1_rs.at[src], (g, src, d)
        ).wait_recv()

    big[...] = mm_nt(att_tok[...], wo[...])
    gate_row = mod[2]

    @pl.loop(0, TOK // 16)
    def _(i):
        rows = pl.ds(pl.multiple_of(i * 16, 16), 16)
        mixed = hid[rows, :].astype(F32) + gate_row * big[rows, :]
        y, r = norm_rows(mixed)
        fin[rows, :] = y
        rstd[rows, :] = jnp.broadcast_to(r, (16, 128))
        tokbf[rows, :] = y.astype(BF16)

    step = jnp.full((TOK, 64), steps[0], jnp.int32).astype(F32)
    angle = (step / 1000 + 0.008) / 1.008 * (math.pi / 2)
    target = jnp.cos(angle) * noise[...].T - jnp.sin(angle) * ltok[:, 0:64]
    pred_grad = ((2.0 / 64) * (mm_nt(tokbf[...], wp[...]) - target)).astype(BF16)
    big[...] = mm(pred_grad, wp[...])

    @pl.loop(0, TOK // 16)
    def _(i):
        rows = pl.ds(pl.multiple_of(i * 16, 16), 16)
        dy = big[rows, :]
        y = fin[rows, :]
        mean_dy = jnp.mean(dy, axis=-1, keepdims=True)
        mean_dyy = jnp.mean(dy * y, axis=-1, keepdims=True)
        dx = (dy - mean_dy - y * mean_dyy) * rstd[rows, 0:1]
        tokbf[rows, :] = (gate_row * dx).astype(BF16)

    ag_tok[...] = mm(tokbf[...], wo[...]).astype(BF16)

    def ag_copy(j):
        peer = lax.rem(s + j, NS)
        return remote(
            ag_tok.at[:, cols(peer)], ag_head.at[cols(s), :], a2_ss.at[j], a2_rs.at[s], (g, peer, d)
        )

    @pl.loop(1, 8)
    def _(j):
        ag_copy(j).start()

    ag_head[cols(s), :] = ag_tok[:, cols(s)]

    @pl.loop(1, 8)
    def _(j):
        src = lax.rem(s + 8 - j, NS)
        remote(
            ag_tok.at[:, cols(src)], ag_head.at[cols(src), :], a2_ss.at[j], a2_rs.at[src], (g, src, d)
        ).wait_recv()

    @pl.loop(0, 8)
    def _(j):
        here = cols(j)
        val = ag_head[here, :].astype(F32).T
        agT[:, here] = val.astype(BF16)
        num[:, here] = val * attT[:, here].astype(F32)

    deltas = [jnp.sum(num[h * 64 : h * 64 + 64, :], axis=0, keepdims=True) for h in range(2)]
    invs = [1.0 / tots[h] for h in range(2)]
    dqT[...] = jnp.zeros_like(dqT)
    low_k = lax.broadcasted_iota(jnp.int32, (KB, 128), 1) < 64

    @pl.loop(0, S // KB)
    def _(c):
        rows = cols(c, KB)
        dvs = []
        dks = []
        for h in range(2):
            p = eT[h, rows, :] * invs[h]
            dp = mm(vmask[h, rows, :], agT[...])
            ds = (p * (dp - deltas[h])).astype(BF16)
            dvs.append(mm(p.astype(BF16), ag_head[...]))
            dks.append(mm(ds, qrow[...]))
            hr = slice(h * 64, h * 64 + 64)
            dqT[hr, :] += mm(kT[hr, rows], ds)
        dv[rows, :] = jnp.where(low_k, dvs[0], dvs[1])
        dk[rows, :] = jnp.where(low_k, dks[0], dks[1]) * 0.125

    def ig_copy(j):
        here = cols(j)
        return remote(
            ig.at[here, :], ig_sib.at[here, :], sb_ss.at[j], sb_rs.at[j], (1 - g, s, d)
        )

    @pl.loop(0, 8)
    def _(j):
        here = cols(j)
        grad = head_norm_back_t(dqT[:, here] * 0.125 * gq, xq[:, here], rq[:, here])
        ig[here, 0:128] = grad.T.astype(BF16)
        grad = head_norm_back_t(dk[here, :].T * gk, xk[:, here], rk[:, here])
        ig[here, 128:256] = grad.T.astype(BF16)
        ig[here, 256:384] = dv[here, :].astype(BF16)
        ig_copy(j).start()

    def dp_copy(c):
        return remote(wg_own.at[c], dpr.at[d], dp_ss.at[c], dp_rs.at[d], (g, s, c))

    @pl.loop(0, 8)
    def _(j):
        ig_copy(j).wait_recv()

    norm_copy.wait_recv()

    @pl.loop(0, 4)
    def _(j):
        i = lax.rem(d // 2 + 1 + j, 4)
        rows = pl.ds(pl.multiple_of(g * HALF + i * 240, 16), 240)
        value = mm(nT[rows, :], ig[...])
        value = value + mm(nT_sib[pl.ds(pl.multiple_of(i * 240, 16), 240), :], ig_sib[...])
        for q in range(2):
            c = 2 * i + q
            wg_own[c] = value[q * PART : q * PART + PART]

            @pl.when(c != d)
            def _():
                dp_copy(c).start()

    acc[PART:, :] = jnp.zeros((128 - PART, W3), F32)
    acc[0:PART, :] = wg_own[d]

    @pl.loop(1, 8)
    def _(j):
        src = lax.rem(d + 8 - j, ND)
        remote(wg_own.at[src], dpr.at[src], dp_ss.at[src], dp_rs.at[src], (g, s, src)).wait_recv()
        acc[0:PART, :] += dpr[src]

    for j in range(8):
        fsend[j] = acc[j * OUT_ROWS : j * OUT_ROWS + 16, :]

    def fin_copy(j):
        return remote(fsend.at[j], frecv.at[s], fn_ss.at[j], fn_rs.at[s], (g, d, j))

    @pl.loop(0, 8)
    def _(j):
        me = jnp.logical_and(s == d, j == d)

        @pl.when(me)
        def _():
            frecv[s] = fsend[j]

        @pl.when(jnp.logical_not(me))
        def _():
            fin_copy(j).start()

    @pl.loop(0, 8)
    def _(j):
        me = jnp.logical_and(s == d, j == d)

        @pl.when(jnp.logical_not(me))
        def _():
            remote(fsend.at[j], frecv.at[j], fn_ss.at[j], fn_rs.at[j], (g, j, s)).wait_recv()

    for j in range(8):
        for part in range(3):
            out_ref[:, part * INNER + j * 128 : part * INNER + j * 128 + 128] = frecv[
                j, 0:OUT_ROWS, part * 128 : part * 128 + 128
            ]

    for copy in own_sends:
        copy.wait_send()

    @pl.loop(6, 14)
    def _(sem):
        pass_on(0, 0, sem, z_up).wait_send()

    @pl.loop(1, 8)
    def _(j):
        att_copy(j).wait_send()
        ag_copy(j).wait_send()

    @pl.loop(0, 8)
    def _(j):
        ig_copy(j).wait_send()

    @pl.loop(1, 16)
    def _(j):
        latent_copy(j).wait_send()

    norm_copy.wait_send()

    @pl.loop(0, 8)
    def _(c):
        @pl.when(c != d)
        def _():
            dp_copy(c).wait_send()

        me = jnp.logical_and(s == d, c == d)

        @pl.when(jnp.logical_not(me))
        def _():
            fin_copy(c).wait_send()


def scratch_shapes():
    V = pltpu.VMEM
    dma = pltpu.SemaphoreType.DMA
    return [
        V((512, C), BF16),
        V((432, C), BF16),
        V((TOK, D), BF16),
        V((64, TOK), F32),
        V((D, W3), BF16),
        V((D, INNER), BF16),
        V((64, D), BF16),
        V((NS, TOK, D), BF16),
        V((D, S), BF16),
        V((W3, D), BF16),
        V((512, W3), F32),
        V((16, 32, 128), F32),
        V((16, 32, 128), F32),
        V((512, 128), F32),
        V((TOK, 128), F32),
        V((128, S), BF16),
        V((128, S), BF16),
        V((128, S), BF16),
        V((S, 128), BF16),
        V((2, S, 128), BF16),
        V((2, S, 128), BF16),
        V((128, S), F32),
        V((128, S), F32),
        V((2, S), F32),
        V((2, S), F32),
        V((2, S, S), F32),
        V((128, S), F32),
        V((128, S), BF16),
        V((S, 128), BF16),
        V((TOK, INNER), BF16),
        V((TOK, D), F32),
        V((TOK, D), F32),
        V((TOK, 128), F32),
        V((TOK, D), BF16),
        V((TOK, INNER), BF16),
        V((S, 128), BF16),
        V((128, S), BF16),
        V((128, S), F32),
        V((S, 128), F32),
        V((S, 128), F32),
        V((S, W3), BF16),
        V((S, W3), BF16),
        V((HALF, S), BF16),
        V((8, PART, W3), F32),
        V((8, PART, W3), F32),
        V((128, W3), F32),
        V((8, 16, W3), F32),
        V((8, 16, W3), F32),
        dma((9,)),
        dma((14,)),
        dma((16,)),
        dma((16,)),
        dma((16,)),
        dma((8,)),
        dma((8,)),
        dma((8,)),
        dma((8,)),
        dma((8,)),
        dma((8,)),
        dma((8,)),
        dma((8,)),
        dma((8,)),
        dma((8,)),
        dma((2,)),
    ]


def local(
    features,
    group_gain,
    group_bias,
    conv_weight,
    hidden,
    modulation,
    timesteps,
    fresh_noise,
    input_weight,
    query_gain,
    key_gain,
    output_weight,
    patch_weight,
):
    vmem = pl.BlockSpec(memory_space=pltpu.VMEM)
    hbm = pl.BlockSpec(memory_space=pl.ANY)
    return pl.pallas_call(
        kernel,
        out_shape=jax.ShapeDtypeStruct((OUT_ROWS, 3 * INNER), F32),
        in_specs=[pl.BlockSpec(memory_space=pltpu.SMEM)] + [vmem] * 5 + [hbm] * 7,
        out_specs=vmem,
        scratch_shapes=scratch_shapes(),
        compiler_params=pltpu.CompilerParams(
            collective_id=0, has_side_effects=True, vmem_limit_bytes=60 * 2**20
        ),
    )(
        timesteps.reshape(1),
        group_gain.reshape(1, C),
        group_bias.reshape(1, C),
        modulation.reshape(3, 1, D),
        query_gain.reshape(1, 64),
        key_gain.reshape(1, 64),
        features.reshape(512, C),
        conv_weight.T,
        hidden.reshape(TOK, D),
        fresh_noise.reshape(TOK, 64).T,
        input_weight,
        output_weight,
        patch_weight.T,
    )


def solution(mesh):
    in_specs = (
        P("dp", None, None, ("grp", "seq"), None, None),
        P(),
        P(),
        P(),
        P("grp", None, "dp", "seq", None),
        P("grp", None, "dp", None, None),
        P("grp", None, "dp"),
        P("grp", None, "dp", "seq", None),
        P(),
        P(),
        P(),
        P(),
        P(),
    )
    out_specs = P(("grp", "seq", "dp"), None)
    return jax.shard_map(local, mesh=mesh, in_specs=in_specs, out_specs=out_specs, check_vma=False)
```

```python
import math

import jax
import jax.numpy as jnp
from jax import lax
from jax.experimental import pallas as pl
from jax.experimental.pallas import tpu as pltpu
from jax.sharding import PartitionSpec as P

F32 = jnp.float32
BF16 = jnp.bfloat16
MESH = pl.DeviceIdType.MESH

NG, NS, ND = 2, 8, 8
D = 1920
INNER = 1024
S = 1024
TOK = 128
W3 = 384
C = 512
HALF = D // NG
PART = HALF // ND
OUT_ROWS = 15
KB = 256
LATENT_SCALE = 1.15258426
GROUP_EPS = 1e-06
LAYER_EPS = 1e-05
HEAD_EPS = 1e-06


def mm(a, b):
    return lax.dot_general(a, b, (((1,), (0,)), ((), ())), preferred_element_type=F32)


def mm_nt(a, b):
    return lax.dot_general(a, b, (((1,), (1,)), ((), ())), preferred_element_type=F32)


def norm_rows(x):
    mu = jnp.mean(x, axis=-1, keepdims=True)
    centred = x - mu
    var = jnp.mean(centred * centred, axis=-1, keepdims=True)
    r = lax.rsqrt(var + LAYER_EPS)
    return centred * r, r


def head_norm_t(x):
    x3 = x.reshape(2, 64, x.shape[1])
    mu = jnp.mean(x3, axis=1, keepdims=True)
    centred = x3 - mu
    var = jnp.mean(centred * centred, axis=1, keepdims=True)
    r = lax.rsqrt(var + HEAD_EPS)
    return (centred * r).reshape(x.shape), r[:, 0, :]


def head_norm_back_t(grad, xhat, r):
    g3 = grad.reshape(2, 64, grad.shape[1])
    x3 = xhat.reshape(2, 64, grad.shape[1])
    mean_g = jnp.mean(g3, axis=1, keepdims=True)
    mean_gx = jnp.mean(g3 * x3, axis=1, keepdims=True)
    return ((g3 - mean_g - x3 * mean_gx) * r[:, None, :]).reshape(grad.shape)


def gain_columns(gain_row):
    both = jnp.concatenate([gain_row, gain_row], axis=1)
    return jnp.broadcast_to(both, (128, 128)).T


def group_mean(v, count):
    lane = lax.broadcasted_iota(jnp.int32, v.shape, 1)
    for step in (1, 2, 4, 8):
        up = pltpu.roll(v, C - step, 1)
        down = pltpu.roll(v, step, 1)
        v = v + jnp.where((lane & step) == 0, up, down)
    return v * (1.0 / count)


def kernel(
    steps,
    ggain,
    gbias,
    mod,
    qgain,
    kgain,
    feat_hbm,
    cw_hbm,
    hid_hbm,
    noise_hbm,
    w_hbm,
    wo_hbm,
    wp_hbm,
    out_ref,
    feat,
    cw,
    hid,
    noise,
    wq,
    wo,
    wp,
    ng,
    nT,
    wqT,
    taps,
    vsend,
    vrecv,
    lat,
    ltok,
    qT,
    kT,
    vT,
    qrow,
    kmask,
    vmask,
    xq,
    xk,
    rq,
    rk,
    eT,
    num,
    attT,
    att_row,
    att_tok,
    big,
    fin,
    rstd,
    tokbf,
    ag_tok,
    ag_head,
    agT,
    dqT,
    dk,
    ig,
    ig_sib,
    igv,
    igv_sib,
    nT_sib,
    invs,
    wgv,
    wgq,
    dpv,
    dpq,
    accv,
    accq,
    fsv,
    fsq,
    frv,
    frq,
    ld_sem,
    ag_ss,
    ag_rs,
    lt_ss,
    lt_rs,
    a1_ss,
    a1_rs,
    a2_ss,
    a2_rs,
    sb_ss,
    sb_rs,
    sv_ss,
    sv_rs,
    dv_ss,
    dv_rs,
    dq_ss,
    dq_rs,
    fv_ss,
    fv_rs,
    fq_ss,
    fq_rs,
    nt_sem,
):
    g = lax.axis_index("grp")
    s = lax.axis_index("seq")
    d = lax.axis_index("dp")
    tile = g * NS + s

    def remote(src, dst, ssem, rsem, dev):
        return pltpu.make_async_remote_copy(
            src_ref=src, dst_ref=dst, send_sem=ssem, recv_sem=rsem, device_id=dev, device_id_type=MESH
        )

    def cols(index, width=128):
        return pl.ds(pl.multiple_of(index * width, width), width)

    loads = [
        pltpu.make_async_copy(hid_hbm, hid, ld_sem.at[0]),
        pltpu.make_async_copy(feat_hbm, feat, ld_sem.at[1]),
        pltpu.make_async_copy(cw_hbm, cw, ld_sem.at[2]),
        pltpu.make_async_copy(w_hbm.at[:, cols(s)], wq.at[:, 0:128], ld_sem.at[3]),
        pltpu.make_async_copy(w_hbm.at[:, cols(s + 8)], wq.at[:, 128:256], ld_sem.at[4]),
        pltpu.make_async_copy(w_hbm.at[:, cols(s + 16)], wq.at[:, 256:384], ld_sem.at[5]),
        pltpu.make_async_copy(noise_hbm, noise, ld_sem.at[6]),
        pltpu.make_async_copy(wo_hbm, wo, ld_sem.at[7]),
        pltpu.make_async_copy(wp_hbm, wp, ld_sem.at[8]),
    ]
    for copy in loads:
        copy.start()

    barrier = pltpu.get_barrier_semaphore()

    def greet(dev):
        pl.semaphore_signal(barrier, inc=1, device_id=dev, device_id_type=MESH)

    @pl.loop(1, 16)
    def _(j):
        t = lax.rem(tile + j, 16)
        greet((t // NS, lax.rem(t, NS), d))

    @pl.loop(1, 8)
    def _(j):
        greet((g, s, lax.rem(d + j, ND)))

    @pl.loop(0, 8)
    def _(j):
        me = jnp.logical_and(s == d, j == d)

        @pl.when(jnp.logical_not(me))
        def _():
            greet((g, d, j))
            greet((g, j, s))

    loads[0].wait()
    shift_row = mod[0]
    scale_row = 1.0 + mod[1]

    @pl.loop(0, TOK // 16)
    def _(i):
        rows = pl.ds(pl.multiple_of(i * 16, 16), 16)
        y, _ = norm_rows(hid[rows, :].astype(F32))
        ng[s, rows, :] = (y * scale_row + shift_row).astype(BF16)

    selfs = jnp.where(s == d, 2, 0)
    pl.semaphore_wait(barrier, 15 + 7 + 16 - selfs)

    yh, z = s // 4, lax.rem(s, 4)
    z_up = yh * 4 + lax.rem(z + 1, 4)
    z_down = yh * 4 + lax.rem(z + 3, 4)
    across = (1 - yh) * 4 + z

    def pass_on(slot, half, sem, peer):
        block = ng.at[slot, pl.ds(half * 64, 64), :]
        return remote(block, block, ag_ss.at[sem], ag_rs.at[slot * 2 + half], (g, peer, d))

    own_sends = [
        pass_on(s, half, half * 3 + k, peer)
        for half in range(2)
        for k, peer in enumerate((z_up, z_down, across))
    ]
    for copy in own_sends:
        copy.start()

    loads[1].wait()
    loads[2].wait()
    row_id = lax.broadcasted_iota(jnp.int32, (W3, 432), 1)
    col_id = lax.broadcasted_iota(jnp.int32, (W3, 432), 0)
    inner = col_id & 127
    src0 = (col_id >> 7) * 144 + (inner >> 4) * 48 + (inner & 15)
    used = inner < 48
    cw_val = cw[...]
    col_w = lax.broadcasted_iota(jnp.int32, (C, C), 0) & 15
    acts = []
    for clip in range(2):
        x = feat[clip * 256 : clip * 256 + 256, :].astype(F32)
        mean = group_mean(jnp.broadcast_to(jnp.sum(x, axis=0, keepdims=True), (8, C)), 4096.0)[0:1]
        centred = x - mean
        var = group_mean(
            jnp.broadcast_to(jnp.sum(centred * centred, axis=0, keepdims=True), (8, C)), 4096.0
        )[0:1]
        normed = centred * lax.rsqrt(var + GROUP_EPS) * ggain[...] + gbias[...]
        acts.append(normed / (1.0 + jnp.exp(-normed)))
    act = jnp.concatenate(acts, axis=0)
    for e in range(3):
        pick = jnp.where(jnp.logical_and(used, row_id == src0 + e * 16), 1.0, 0.0).astype(BF16)
        we = mm(pick, cw_val).astype(BF16)
        if e == 0:
            ae = jnp.where(col_w == 0, 0.0, pltpu.roll(act, 1, 0))
        elif e == 2:
            ae = jnp.where(col_w == 15, 0.0, pltpu.roll(act, C - 1, 0))
        else:
            ae = act
        term = mm_nt(ae.astype(BF16), we)
        if e == 0:
            taps[...] = term
        else:
            taps[...] += term
    for clip in range(2):
        for frame in range(8):
            total = None
            for a in range(3):
                base = (clip * 8 + max(frame + a - 2, 0)) * 32
                piece = taps[base : base + 32, a * 128 : a * 128 + 128]
                total = piece if total is None else total + piece
            vsend[clip * 8 + frame] = total
    vrecv[tile] = vsend[tile]

    def latent_copy(j):
        t = lax.rem(tile + j, 16)
        return remote(
            vsend.at[t], vrecv.at[tile], lt_ss.at[j], lt_rs.at[tile], (t // NS, lax.rem(t, NS), d)
        )

    @pl.loop(1, 16)
    def _(j):
        latent_copy(j).start()

    loads[3].wait()
    loads[4].wait()
    loads[5].wait()

    @pl.loop(0, 15)
    def _(i):
        wqT[:, cols(i)] = wq[cols(i), :].T

    gq = gain_columns(qgain[...])
    gk = gain_columns(kgain[...])
    low = lax.broadcasted_iota(jnp.int32, (128, 128), 1) < 64

    @pl.loop(0, 8)
    def _(j):
        other = jnp.logical_or(j == 3, j >= 5)
        hop = jnp.where(
            jnp.logical_or(j == 1, j == 5), 3, jnp.where(jnp.logical_or(j == 2, j == 6), 1, 0)
        )
        hop = jnp.where(jnp.logical_or(j == 4, j == 7), 2, hop)
        src = jnp.where(other, 1 - yh, yh) * 4 + lax.rem(z + hop, 4)

        @pl.when(j > 0)
        def _():
            for half in range(2):
                pass_on(src, half, 0, z_up).wait_recv()

                if half == 0:

                    @pl.when(j == 1)
                    def _():
                        pass_on(src, 0, 6, z_up).start()

                else:

                    @pl.when(j == 2)
                    def _():
                        pass_on(src, 1, 7, z_down).start()

                @pl.when(j == 3)
                def _():
                    pass_on(src, half, 8 + 2 * half, z_up).start()
                    pass_on(src, half, 9 + 2 * half, z_down).start()

                @pl.when(j == 4)
                def _():
                    pass_on(src, half, 12 + half, across).start()

        here = cols(src)
        nt = ng[src].T
        nT[:, here] = nt
        pT = mm(wqT[...], nt)
        xhat, r = head_norm_t(pT[0:128])
        xq[:, here] = xhat
        rq[:, here] = r
        val = xhat * gq
        qT[:, here] = val.astype(BF16)
        qrow[here, :] = val.T.astype(BF16)
        xhat, r = head_norm_t(pT[128:256])
        xk[:, here] = xhat
        rk[:, here] = r
        val = xhat * gk
        kT[:, here] = val.astype(BF16)
        row = val.T
        kmask[0, here, :] = jnp.where(low, row, 0.0).astype(BF16)
        kmask[1, here, :] = jnp.where(low, 0.0, row).astype(BF16)
        val = pT[256:384]
        vT[:, here] = val.astype(BF16)
        row = val.T
        vmask[0, here, :] = jnp.where(low, row, 0.0).astype(BF16)
        vmask[1, here, :] = jnp.where(low, 0.0, row).astype(BF16)

    norm_copy = remote(
        nT.at[pl.ds(pl.multiple_of((1 - g) * HALF, 16), HALF), :],
        nT_sib,
        nt_sem.at[0],
        nt_sem.at[1],
        (1 - g, s, d),
    )
    norm_copy.start()

    def att_copy(peer):
        return remote(
            att_row.at[cols(peer), :],
            att_tok.at[:, cols(s)],
            a1_ss.at[peer],
            a1_rs.at[s],
            (g, peer, d),
        )

    @pl.loop(0, S // KB)
    def _(j):
        c = lax.rem(s // 2 + 1 + j, S // KB)
        here = cols(c, KB)
        for h in range(2):
            hr = slice(h * 64, h * 64 + 64)
            e = jnp.exp(mm(kmask[h], qT[:, here]) * 0.125)
            eT[h, :, here] = e
            inv = 1.0 / jnp.sum(e, axis=0, keepdims=True)
            invs[h : h + 1, here] = inv
            num[hr, here] = mm(vT[hr, :], e.astype(BF16)) * inv
        val = num[:, here]
        attT[:, here] = val.astype(BF16)
        att_row[here, :] = val.T.astype(BF16)
        for q in range(2):
            peer = 2 * c + q

            @pl.when(peer != s)
            def _():
                att_copy(peer).start()

    att_tok[:, cols(s)] = att_row[cols(s), :]

    @pl.loop(1, 16)
    def _(j):
        t = lax.rem(tile + j, 16)
        remote(
            vsend.at[t], vrecv.at[t], lt_ss.at[j], lt_rs.at[t], (t // NS, lax.rem(t, NS), d)
        ).wait_recv()

    x = vrecv[...].reshape(512, 128)
    pad = jnp.zeros((16, 128), F32)
    total = jnp.concatenate([pad, x[:-16]], axis=0) + pltpu.roll(x, 112, 1)
    total = total + jnp.concatenate([pltpu.roll(x, 96, 1)[16:], pad], axis=0)
    lane = lax.broadcasted_iota(jnp.int32, (512, 128), 1)
    lat[...] = jnp.where(lane < 16, total * LATENT_SCALE, 0.0)
    tokens = jnp.zeros((128, 128), F32)
    for jj in range(2):
        half = lat[pl.ds(jj, 256, stride=2), :].reshape(16, 2, 8, 128)
        for ii in range(2):
            piece = half[:, ii].reshape(128, 128)
            place = 16 * (2 * ii + jj)
            tokens = tokens + (pltpu.roll(piece, place, 1) if place else piece)
    ltok[...] = tokens

    for index in (6, 7, 8):
        loads[index].wait()

    @pl.loop(1, 8)
    def _(j):
        src = lax.rem(s + 8 - j, NS)
        remote(
            att_row.at[cols(src), :], att_tok.at[:, cols(src)], a1_ss.at[src], a1_rs.at[src], (g, src, d)
        ).wait_recv()

    big[...] = mm_nt(att_tok[...], wo[...])
    gate_row = mod[2]

    @pl.loop(0, TOK // 16)
    def _(i):
        rows = pl.ds(pl.multiple_of(i * 16, 16), 16)
        mixed = hid[rows, :].astype(F32) + gate_row * big[rows, :]
        y, r = norm_rows(mixed)
        fin[rows, :] = y
        rstd[rows, :] = jnp.broadcast_to(r, (16, 128))
        tokbf[rows, :] = y.astype(BF16)

    step = jnp.full((TOK, 64), steps[0], jnp.int32).astype(F32)
    angle = (step / 1000 + 0.008) / 1.008 * (math.pi / 2)
    target = jnp.cos(angle) * noise[...].T - jnp.sin(angle) * ltok[:, 0:64]
    pred_grad = ((2.0 / 64) * (mm_nt(tokbf[...], wp[...]) - target)).astype(BF16)
    big[...] = mm(pred_grad, wp[...])

    @pl.loop(0, TOK // 16)
    def _(i):
        rows = pl.ds(pl.multiple_of(i * 16, 16), 16)
        dy = big[rows, :]
        y = fin[rows, :]
        mean_dy = jnp.mean(dy, axis=-1, keepdims=True)
        mean_dyy = jnp.mean(dy * y, axis=-1, keepdims=True)
        dx = (dy - mean_dy - y * mean_dyy) * rstd[rows, 0:1]
        tokbf[rows, :] = (gate_row * dx).astype(BF16)

    ag_tok[...] = mm(tokbf[...], wo[...]).astype(BF16)

    def ag_copy(j):
        peer = lax.rem(s + j, NS)
        return remote(
            ag_tok.at[:, cols(peer)], ag_head.at[cols(s), :], a2_ss.at[j], a2_rs.at[s], (g, peer, d)
        )

    @pl.loop(1, 8)
    def _(j):
        ag_copy(j).start()

    ag_head[cols(s), :] = ag_tok[:, cols(s)]

    @pl.loop(1, 8)
    def _(j):
        src = lax.rem(s + 8 - j, NS)
        remote(
            ag_tok.at[:, cols(src)], ag_head.at[cols(src), :], a2_ss.at[j], a2_rs.at[src], (g, src, d)
        ).wait_recv()

    @pl.loop(0, 8)
    def _(j):
        here = cols(j)
        val = ag_head[here, :].astype(F32).T
        agT[:, here] = val.astype(BF16)
        num[:, here] = val * attT[:, here].astype(F32)

    def v_copy(c):
        rows = cols(c, KB)
        return remote(
            igv.at[rows, :], igv_sib.at[rows, :], sv_ss.at[c], sv_rs.at[c], (1 - g, s, d)
        )

    low_k = lax.broadcasted_iota(jnp.int32, (KB, 128), 1) < 64

    @pl.loop(0, S // KB)
    def _(c):
        rows = cols(c, KB)
        dvs = []
        for h in range(2):
            p = eT[h, rows, :] * invs[h : h + 1, :]
            dvs.append(mm(p.astype(BF16), ag_head[...]))
        igv[rows, :] = jnp.where(low_k, dvs[0], dvs[1]).astype(BF16)
        v_copy(c).start()

    deltas = [jnp.sum(num[h * 64 : h * 64 + 64, :], axis=0, keepdims=True) for h in range(2)]
    dqT[...] = jnp.zeros_like(dqT)

    def score_back(c):
        rows = cols(c, KB)
        dks = []
        for h in range(2):
            p = eT[h, rows, :] * invs[h : h + 1, :]
            dp = mm(vmask[h, rows, :], agT[...])
            ds = (p * (dp - deltas[h])).astype(BF16)
            dks.append(mm(ds, qrow[...]))
            hr = slice(h * 64, h * 64 + 64)
            dqT[hr, :] += mm(kT[hr, rows], ds)
        dk[rows, :] = jnp.where(low_k, dks[0], dks[1]) * 0.125

    @pl.loop(0, 2)
    def _(c):
        score_back(c)

    def grad_rows(i, mine, theirs):
        rows = pl.ds(pl.multiple_of(g * HALF + i * 240, 16), 240)
        value = mm(nT[rows, :], mine[...])
        return value + mm(nT_sib[pl.ds(pl.multiple_of(i * 240, 16), 240), :], theirs[...])

    def dpv_copy(c):
        return remote(wgv.at[c], dpv.at[d], dv_ss.at[c], dv_rs.at[d], (g, s, c))

    def dpq_copy(c):
        return remote(wgq.at[c], dpq.at[d], dq_ss.at[c], dq_rs.at[d], (g, s, c))

    norm_copy.wait_recv()

    @pl.loop(0, S // KB)
    def _(c):
        v_copy(c).wait_recv()

    @pl.loop(0, 4)
    def _(j):
        i = lax.rem(d // 2 + 1 + j, 4)
        value = grad_rows(i, igv, igv_sib)
        for q in range(2):
            c = 2 * i + q
            wgv[c] = value[q * PART : q * PART + PART]

            @pl.when(c != d)
            def _():
                dpv_copy(c).start()

    @pl.loop(2, 4)
    def _(c):
        score_back(c)

    def ig_copy(j):
        here = cols(j)
        return remote(
            ig.at[here, :], ig_sib.at[here, :], sb_ss.at[j], sb_rs.at[j], (1 - g, s, d)
        )

    @pl.loop(0, 8)
    def _(j):
        here = cols(j)
        grad = head_norm_back_t(dqT[:, here] * 0.125 * gq, xq[:, here], rq[:, here])
        ig[here, 0:128] = grad.T.astype(BF16)
        grad = head_norm_back_t(dk[here, :].T * gk, xk[:, here], rk[:, here])
        ig[here, 128:256] = grad.T.astype(BF16)
        ig_copy(j).start()

    @pl.loop(0, 8)
    def _(j):
        ig_copy(j).wait_recv()

    @pl.loop(0, 4)
    def _(j):
        i = lax.rem(d // 2 + 1 + j, 4)
        value = grad_rows(i, ig, ig_sib)
        for q in range(2):
            c = 2 * i + q
            wgq[c] = value[q * PART : q * PART + PART]

            @pl.when(c != d)
            def _():
                dpq_copy(c).start()

    def finish_columns(own, arrived, part_sem, total, out_send, out_recv, send_sem, recv_sem):
        total[PART:, :] = jnp.zeros((128 - PART, total.shape[1]), F32)
        total[0:PART, :] = own[d]

        @pl.loop(1, 8)
        def _(j):
            src = lax.rem(d + 8 - j, ND)
            remote(own.at[src], arrived.at[src], part_sem.at[src], part_sem.at[src], (g, s, src)).wait_recv()
            total[0:PART, :] += arrived[src]

        for j in range(8):
            out_send[j] = total[j * OUT_ROWS : j * OUT_ROWS + 16, :]

        @pl.loop(0, 8)
        def _(j):
            me = jnp.logical_and(s == d, j == d)

            @pl.when(me)
            def _():
                out_recv[s] = out_send[j]

            @pl.when(jnp.logical_not(me))
            def _():
                remote(
                    out_send.at[j], out_recv.at[s], send_sem.at[j], recv_sem.at[s], (g, d, j)
                ).start()

    finish_columns(wgv, dpv, dv_rs, accv, fsv, frv, fv_ss, fv_rs)
    finish_columns(wgq, dpq, dq_rs, accq, fsq, frq, fq_ss, fq_rs)

    @pl.loop(0, 8)
    def _(j):
        me = jnp.logical_and(s == d, j == d)

        @pl.when(jnp.logical_not(me))
        def _():
            remote(fsv.at[j], frv.at[j], fv_ss.at[j], fv_rs.at[j], (g, j, s)).wait_recv()
            remote(fsq.at[j], frq.at[j], fq_ss.at[j], fq_rs.at[j], (g, j, s)).wait_recv()

    for j in range(8):
        lanes = slice(j * 128, j * 128 + 128)
        out_ref[:, lanes] = frq[j, 0:OUT_ROWS, 0:128]
        out_ref[:, INNER + j * 128 : INNER + j * 128 + 128] = frq[j, 0:OUT_ROWS, 128:256]
        out_ref[:, 2 * INNER + j * 128 : 2 * INNER + j * 128 + 128] = frv[j, 0:OUT_ROWS, :]

    for copy in own_sends:
        copy.wait_send()

    @pl.loop(6, 14)
    def _(sem):
        pass_on(0, 0, sem, z_up).wait_send()

    @pl.loop(1, 8)
    def _(j):
        att_copy(lax.rem(s + j, NS)).wait_send()
        ag_copy(j).wait_send()

    @pl.loop(0, 8)
    def _(j):
        ig_copy(j).wait_send()

    @pl.loop(0, S // KB)
    def _(c):
        v_copy(c).wait_send()

    @pl.loop(1, 16)
    def _(j):
        latent_copy(j).wait_send()

    norm_copy.wait_send()

    @pl.loop(0, 8)
    def _(c):
        @pl.when(c != d)
        def _():
            dpv_copy(c).wait_send()
            dpq_copy(c).wait_send()

        me = jnp.logical_and(s == d, c == d)

        @pl.when(jnp.logical_not(me))
        def _():
            remote(fsv.at[c], frv.at[s], fv_ss.at[c], fv_rs.at[s], (g, d, c)).wait_send()
            remote(fsq.at[c], frq.at[s], fq_ss.at[c], fq_rs.at[s], (g, d, c)).wait_send()


def scratch_shapes():
    V = pltpu.VMEM
    dma = pltpu.SemaphoreType.DMA
    return [
        V((512, C), BF16),
        V((432, C), BF16),
        V((TOK, D), BF16),
        V((64, TOK), F32),
        V((D, W3), BF16),
        V((D, INNER), BF16),
        V((64, D), BF16),
        V((NS, TOK, D), BF16),
        V((D, S), BF16),
        V((W3, D), BF16),
        V((512, W3), F32),
        V((16, 32, 128), F32),
        V((16, 32, 128), F32),
        V((512, 128), F32),
        V((TOK, 128), F32),
        V((128, S), BF16),
        V((128, S), BF16),
        V((128, S), BF16),
        V((S, 128), BF16),
        V((2, S, 128), BF16),
        V((2, S, 128), BF16),
        V((128, S), F32),
        V((128, S), F32),
        V((2, S), F32),
        V((2, S), F32),
        V((2, S, S), F32),
        V((128, S), F32),
        V((128, S), BF16),
        V((S, 128), BF16),
        V((TOK, INNER), BF16),
        V((TOK, D), F32),
        V((TOK, D), F32),
        V((TOK, 128), F32),
        V((TOK, D), BF16),
        V((TOK, INNER), BF16),
        V((S, 128), BF16),
        V((128, S), BF16),
        V((128, S), F32),
        V((S, 128), F32),
        V((S, 256), BF16),
        V((S, 256), BF16),
        V((S, 128), BF16),
        V((S, 128), BF16),
        V((HALF, S), BF16),
        V((2, S), F32),
        V((8, PART, 128), F32),
        V((8, PART, 256), F32),
        V((8, PART, 128), F32),
        V((8, PART, 256), F32),
        V((128, 128), F32),
        V((128, 256), F32),
        V((8, 16, 128), F32),
        V((8, 16, 256), F32),
        V((8, 16, 128), F32),
        V((8, 16, 256), F32),
        dma((9,)),
        dma((14,)),
        dma((16,)),
        dma((16,)),
        dma((16,)),
        dma((8,)),
        dma((8,)),
        dma((8,)),
        dma((8,)),
        dma((8,)),
        dma((8,)),
        dma((4,)),
        dma((4,)),
        dma((8,)),
        dma((8,)),
        dma((8,)),
        dma((8,)),
        dma((8,)),
        dma((8,)),
        dma((8,)),
        dma((8,)),
        dma((2,)),
    ]


def local(
    features,
    group_gain,
    group_bias,
    conv_weight,
    hidden,
    modulation,
    timesteps,
    fresh_noise,
    input_weight,
    query_gain,
    key_gain,
    output_weight,
    patch_weight,
):
    vmem = pl.BlockSpec(memory_space=pltpu.VMEM)
    hbm = pl.BlockSpec(memory_space=pl.ANY)
    return pl.pallas_call(
        kernel,
        out_shape=jax.ShapeDtypeStruct((OUT_ROWS, 3 * INNER), F32),
        in_specs=[pl.BlockSpec(memory_space=pltpu.SMEM)] + [vmem] * 5 + [hbm] * 7,
        out_specs=vmem,
        scratch_shapes=scratch_shapes(),
        compiler_params=pltpu.CompilerParams(
            collective_id=0, has_side_effects=True, vmem_limit_bytes=60 * 2**20
        ),
    )(
        timesteps.reshape(1),
        group_gain.reshape(1, C),
        group_bias.reshape(1, C),
        modulation.reshape(3, 1, D),
        query_gain.reshape(1, 64),
        key_gain.reshape(1, 64),
        features.reshape(512, C),
        conv_weight.T,
        hidden.reshape(TOK, D),
        fresh_noise.reshape(TOK, 64).T,
        input_weight,
        output_weight,
        patch_weight.T,
    )


def solution(mesh):
    in_specs = (
        P("dp", None, None, ("grp", "seq"), None, None),
        P(),
        P(),
        P(),
        P("grp", None, "dp", "seq", None),
        P("grp", None, "dp", None, None),
        P("grp", None, "dp"),
        P("grp", None, "dp", "seq", None),
        P(),
        P(),
        P(),
        P(),
        P(),
    )
    out_specs = P(("grp", "seq", "dp"), None)
    return jax.shard_map(local, mesh=mesh, in_specs=in_specs, out_specs=out_specs, check_vma=False)
```

```python
import math

import jax
import jax.numpy as jnp
from jax import lax
from jax.experimental import pallas as pl
from jax.experimental.pallas import tpu as pltpu
from jax.sharding import PartitionSpec as P

F32 = jnp.float32
BF16 = jnp.bfloat16
MESH = pl.DeviceIdType.MESH

NG, NS, ND = 2, 8, 8
D = 1920
INNER = 1024
S = 1024
TOK = 128
W3 = 384
C = 512
HALF = D // NG
PART = HALF // ND
OUT_ROWS = 15
KB = 256
LATENT_SCALE = 1.15258426
GROUP_EPS = 1e-06
LAYER_EPS = 1e-05
HEAD_EPS = 1e-06


def mm(a, b):
    return lax.dot_general(a, b, (((1,), (0,)), ((), ())), preferred_element_type=F32)


def mm_nt(a, b):
    return lax.dot_general(a, b, (((1,), (1,)), ((), ())), preferred_element_type=F32)


def norm_rows(x):
    mu = jnp.mean(x, axis=-1, keepdims=True)
    centred = x - mu
    var = jnp.mean(centred * centred, axis=-1, keepdims=True)
    r = lax.rsqrt(var + LAYER_EPS)
    return centred * r, r


def head_norm_t(x):
    x3 = x.reshape(2, 64, x.shape[1])
    mu = jnp.mean(x3, axis=1, keepdims=True)
    centred = x3 - mu
    var = jnp.mean(centred * centred, axis=1, keepdims=True)
    r = lax.rsqrt(var + HEAD_EPS)
    return (centred * r).reshape(x.shape), r[:, 0, :]


def head_norm_back_t(grad, xhat, r):
    g3 = grad.reshape(2, 64, grad.shape[1])
    x3 = xhat.reshape(2, 64, grad.shape[1])
    mean_g = jnp.mean(g3, axis=1, keepdims=True)
    mean_gx = jnp.mean(g3 * x3, axis=1, keepdims=True)
    return ((g3 - mean_g - x3 * mean_gx) * r[:, None, :]).reshape(grad.shape)


def gain_columns(gain_row):
    both = jnp.concatenate([gain_row, gain_row], axis=1)
    return jnp.broadcast_to(both, (128, 128)).T


def group_mean(v, count):
    lane = lax.broadcasted_iota(jnp.int32, v.shape, 1)
    for step in (1, 2, 4, 8):
        up = pltpu.roll(v, C - step, 1)
        down = pltpu.roll(v, step, 1)
        v = v + jnp.where((lane & step) == 0, up, down)
    return v * (1.0 / count)


def kernel(
    steps,
    ggain,
    gbias,
    mod,
    qgain,
    kgain,
    feat_hbm,
    cw_hbm,
    hid_hbm,
    noise_hbm,
    w_hbm,
    wo_hbm,
    wp_hbm,
    out_ref,
    feat,
    cw,
    hid,
    noise,
    wq,
    wo,
    wp,
    ng,
    nT,
    wqT,
    qkv_send,
    qkvT,
    r_send,
    r_all,
    taps,
    vsend,
    vrecv,
    lat,
    ltok,
    qrow,
    kmask,
    vmask,
    eT,
    num,
    attT,
    att_row,
    att_tok,
    big,
    fin,
    rstd,
    tokbf,
    ag_tok,
    ag_head,
    agT,
    dqT,
    dk,
    ig,
    ig_sib,
    igv,
    igv_sib,
    nT_sib,
    invs,
    wgv,
    wgq,
    dpv,
    dpq,
    accv,
    accq,
    fsv,
    fsq,
    frv,
    frq,
    ld_sem,
    ag_ss,
    ag_rs,
    lt_ss,
    lt_rs,
    a1_ss,
    a1_rs,
    a2_ss,
    a2_rs,
    sb_ss,
    sb_rs,
    sv_ss,
    sv_rs,
    dv_ss,
    dv_rs,
    dq_ss,
    dq_rs,
    fv_ss,
    fv_rs,
    fq_ss,
    fq_rs,
    nt_ss,
    nt_rs,
    w_sem,
    q_ss,
    q_rs,
    r_ss,
    r_rs,
):
    g = lax.axis_index("grp")
    s = lax.axis_index("seq")
    d = lax.axis_index("dp")
    tile = g * NS + s

    def remote(src, dst, ssem, rsem, dev):
        return pltpu.make_async_remote_copy(
            src_ref=src, dst_ref=dst, send_sem=ssem, recv_sem=rsem, device_id=dev, device_id_type=MESH
        )

    def cols(index, width=128):
        return pl.ds(pl.multiple_of(index * width, width), width)

    yh, z = s // 4, lax.rem(s, 4)
    over = (1 - yh) * 4
    across = over + z
    w_loads = [
        pltpu.make_async_copy(
            w_hbm.at[:, cols(owner + 8 * part)],
            wq.at[:, who * W3 + part * 128 : who * W3 + part * 128 + 128],
            w_sem.at[who * 3 + part],
        )
        for who, owner in enumerate((s, across))
        for part in range(3)
    ]
    hid_load = pltpu.make_async_copy(hid_hbm, hid, ld_sem.at[0])
    hid_load.start()
    for copy in w_loads:
        copy.start()

    loads = [
        hid_load,
        pltpu.make_async_copy(feat_hbm, feat, ld_sem.at[1]),
        pltpu.make_async_copy(cw_hbm, cw, ld_sem.at[2]),
        pltpu.make_async_copy(noise_hbm, noise, ld_sem.at[3]),
        pltpu.make_async_copy(wo_hbm, wo, ld_sem.at[4]),
        pltpu.make_async_copy(wp_hbm, wp, ld_sem.at[5]),
    ]
    for copy in loads[1:]:
        copy.start()

    barrier = pltpu.get_barrier_semaphore()

    def greet(dev):
        pl.semaphore_signal(barrier, inc=1, device_id=dev, device_id_type=MESH)

    @pl.loop(1, 16)
    def _(j):
        t = lax.rem(tile + j, 16)
        greet((t // NS, lax.rem(t, NS), d))

    @pl.loop(1, 8)
    def _(j):
        greet((g, s, lax.rem(d + j, ND)))

    @pl.loop(0, 8)
    def _(j):
        me = jnp.logical_and(s == d, j == d)

        @pl.when(jnp.logical_not(me))
        def _():
            greet((g, d, j))
            greet((g, j, s))

    loads[0].wait()
    shift_row = mod[0]
    scale_row = 1.0 + mod[1]

    @pl.loop(0, TOK // 16, unroll=4)
    def _(i):
        rows = pl.ds(pl.multiple_of(i * 16, 16), 16)
        y, _ = norm_rows(hid[rows, :].astype(F32))
        ng[s, rows, :] = (y * scale_row + shift_row).astype(BF16)

    selfs = jnp.where(s == d, 2, 0)
    pl.semaphore_wait(barrier, 15 + 7 + 16 - selfs)

    z_up = yh * 4 + lax.rem(z + 1, 4)
    z_down = yh * 4 + lax.rem(z + 3, 4)

    def pass_on(slot, half, sem, peer):
        block = ng.at[slot, pl.ds(half * 64, 64), :]
        return remote(block, block, ag_ss.at[sem], ag_rs.at[slot * 2 + half], (g, peer, d))

    def arrived(slot, half):
        pass_on(slot, half, 0, z_up).wait_recv()

    z_two = yh * 4 + lax.rem(z + 2, 4)
    over_up = over + lax.rem(z + 1, 4)
    over_down = over + lax.rem(z + 3, 4)
    over_two = over + lax.rem(z + 2, 4)
    own_sends = [
        pass_on(s, 0, 0, z_up),
        pass_on(s, 1, 1, z_down),
        pass_on(s, 0, 2, across),
        pass_on(s, 1, 3, z_up),
        pass_on(s, 0, 4, z_down),
        pass_on(s, 1, 5, across),
    ]
    for copy in own_sends:
        copy.start()

    loads[1].wait()
    loads[2].wait()
    row_id = lax.broadcasted_iota(jnp.int32, (W3, 432), 1)
    col_id = lax.broadcasted_iota(jnp.int32, (W3, 432), 0)
    inner = col_id & 127
    src0 = (col_id >> 7) * 144 + (inner >> 4) * 48 + (inner & 15)
    used = inner < 48
    cw_val = cw[...]
    col_w = lax.broadcasted_iota(jnp.int32, (C, C), 0) & 15
    acts = []
    for clip in range(2):
        x = feat[clip * 256 : clip * 256 + 256, :].astype(F32)
        mean = group_mean(jnp.broadcast_to(jnp.sum(x, axis=0, keepdims=True), (8, C)), 4096.0)[0:1]
        centred = x - mean
        var = group_mean(
            jnp.broadcast_to(jnp.sum(centred * centred, axis=0, keepdims=True), (8, C)), 4096.0
        )[0:1]
        normed = centred * lax.rsqrt(var + GROUP_EPS) * ggain[...] + gbias[...]
        acts.append(normed / (1.0 + jnp.exp(-normed)))
    act = jnp.concatenate(acts, axis=0)
    for e in range(3):
        pick = jnp.where(jnp.logical_and(used, row_id == src0 + e * 16), 1.0, 0.0).astype(BF16)
        we = mm(pick, cw_val).astype(BF16)
        if e == 0:
            ae = jnp.where(col_w == 0, 0.0, pltpu.roll(act, 1, 0))
        elif e == 2:
            ae = jnp.where(col_w == 15, 0.0, pltpu.roll(act, C - 1, 0))
        else:
            ae = act
        term = mm_nt(ae.astype(BF16), we)
        if e == 0:
            taps[...] = term
        else:
            taps[...] += term
    for clip in range(2):
        for frame in range(8):
            total = None
            for a in range(3):
                base = (clip * 8 + max(frame + a - 2, 0)) * 32
                piece = taps[base : base + 32, a * 128 : a * 128 + 128]
                total = piece if total is None else total + piece
            vsend[clip * 8 + frame] = total
    vrecv[tile] = vsend[tile]

    def latent_copy(j):
        t = lax.rem(tile + j, 16)
        return remote(
            vsend.at[t], vrecv.at[tile], lt_ss.at[j], lt_rs.at[tile], (t // NS, lax.rem(t, NS), d)
        )

    def norm_copy(slot):
        return remote(
            nT.at[pl.ds(pl.multiple_of((1 - g) * HALF, 16), HALF), cols(slot)],
            nT_sib.at[:, cols(slot)],
            nt_ss.at[slot],
            nt_rs.at[slot],
            (1 - g, s, d),
        )

    def take(slot):
        nT[:, cols(slot)] = ng[slot].T
        norm_copy(slot).start()

    for copy in w_loads:
        copy.wait()

    @pl.loop(0, 15)
    def _(i):
        wqT[:, cols(i)] = wq[cols(i), :].T

    gq = gain_columns(qgain[...])
    gk = gain_columns(kgain[...])
    low = lax.broadcasted_iota(jnp.int32, (128, 128), 1) < 64
    r_send[...] = jnp.zeros_like(r_send)

    def hop(j):
        step = jnp.where(j == 1, 3, jnp.where(j == 2, 1, jnp.where(j == 3, 2, 0)))
        return lax.rem(z + step, 4)

    def qkv_copy(j, src):
        return remote(
            qkv_send.at[j], qkvT.at[:, cols(src)], q_ss.at[j], q_rs.at[src], (g, across, d)
        )

    def r_copy(j, src):
        return remote(r_send.at[j], r_all.at[src], r_ss.at[j], r_rs.at[src], (g, across, d))

    def rows_of(here, query, key, value):
        qrow[here, :] = query.T.astype(BF16)
        row = key.T
        kmask[0, here, :] = jnp.where(low, row, 0.0).astype(BF16)
        kmask[1, here, :] = jnp.where(low, 0.0, row).astype(BF16)
        row = value.T
        vmask[0, here, :] = jnp.where(low, row, 0.0).astype(BF16)
        vmask[1, here, :] = jnp.where(low, 0.0, row).astype(BF16)

    @pl.loop(0, 4)
    def _(j):
        src = yh * 4 + hop(j)

        @pl.when(j == 1)
        def _():
            arrived(z_down, 0)
            pass_on(z_down, 0, 6, z_up).start()
            arrived(z_up, 1)
            pass_on(z_up, 1, 7, z_down).start()
            arrived(z_down, 1)

        @pl.when(j == 2)
        def _():
            arrived(z_up, 0)
            for half in range(2):
                arrived(across, half)
                pass_on(across, half, 8 + 2 * half, z_up).start()
                pass_on(across, half, 9 + 2 * half, z_down).start()

        @pl.when(j == 3)
        def _():
            arrived(z_two, 0)
            arrived(z_two, 1)

        here = cols(src)
        take(src)
        pT = mm(wqT[...], nT[:, here])
        for who in (1, 0):
            base = who * W3
            query, rq = head_norm_t(pT[base : base + 128])
            key, rk = head_norm_t(pT[base + 128 : base + 256])
            query = query * gq
            key = key * gk
            value = pT[base + 256 : base + 384]
            if who == 1:
                qkv_send[j, 0:128, :] = query.astype(BF16)
                qkv_send[j, 128:256, :] = key.astype(BF16)
                qkv_send[j, 256:384, :] = value.astype(BF16)
                r_send[j, 0:2, :] = rq
                r_send[j, 2:4, :] = rk
                qkv_copy(j, src).start()
                r_copy(j, src).start()
            else:
                qkvT[0:128, here] = query.astype(BF16)
                qkvT[128:256, here] = key.astype(BF16)
                qkvT[256:384, here] = value.astype(BF16)
                r_all[src, 0:2, :] = rq
                r_all[src, 2:4, :] = rk
                rows_of(here, query, key, value)

    @pl.loop(1, 16)
    def _(j):
        latent_copy(j).start()

    @pl.loop(0, 4)
    def _(j):
        src = over + hop(j)
        qkv_copy(j, src).wait_recv()
        r_copy(j, src).wait_recv()
        here = cols(src)
        rows_of(
            here,
            qkvT[0:128, here].astype(F32),
            qkvT[128:256, here].astype(F32),
            qkvT[256:384, here].astype(F32),
        )

    qT = qkvT.at[0:128]
    kT = qkvT.at[128:256]
    vT = qkvT.at[256:384]

    def att_copy(peer):
        return remote(
            att_row.at[cols(peer), :],
            att_tok.at[:, cols(s)],
            a1_ss.at[peer],
            a1_rs.at[s],
            (g, peer, d),
        )

    @pl.loop(0, S // KB)
    def _(j):
        c = lax.rem(s // 2 + 1 + j, S // KB)
        here = cols(c, KB)
        for h in range(2):
            hr = slice(h * 64, h * 64 + 64)
            e = jnp.exp(mm(kmask[h], qT[:, here]) * 0.125)
            eT[h, :, here] = e
            inv = 1.0 / jnp.sum(e, axis=0, keepdims=True)
            invs[h : h + 1, here] = inv
            num[hr, here] = mm(vT[hr, :], e.astype(BF16)) * inv
        val = num[:, here]
        attT[:, here] = val.astype(BF16)
        att_row[here, :] = val.T.astype(BF16)
        for q in range(2):
            peer = 2 * c + q

            @pl.when(peer != s)
            def _():
                att_copy(peer).start()

    att_tok[:, cols(s)] = att_row[cols(s), :]

    @pl.loop(1, 16)
    def _(j):
        t = lax.rem(tile + j, 16)
        remote(
            vsend.at[t], vrecv.at[t], lt_ss.at[j], lt_rs.at[t], (t // NS, lax.rem(t, NS), d)
        ).wait_recv()

    x = vrecv[...].reshape(512, 128)
    pad = jnp.zeros((16, 128), F32)
    total = jnp.concatenate([pad, x[:-16]], axis=0) + pltpu.roll(x, 112, 1)
    total = total + jnp.concatenate([pltpu.roll(x, 96, 1)[16:], pad], axis=0)
    lane = lax.broadcasted_iota(jnp.int32, (512, 128), 1)
    lat[...] = jnp.where(lane < 16, total * LATENT_SCALE, 0.0)
    tokens = jnp.zeros((128, 128), F32)
    for jj in range(2):
        half = lat[pl.ds(jj, 256, stride=2), :].reshape(16, 2, 8, 128)
        for ii in range(2):
            piece = half[:, ii].reshape(128, 128)
            place = 16 * (2 * ii + jj)
            tokens = tokens + (pltpu.roll(piece, place, 1) if place else piece)
    ltok[...] = tokens

    arrived(over_down, 0)
    pass_on(over_down, 0, 12, z_up).start()
    arrived(over_up, 1)
    pass_on(over_up, 1, 13, z_down).start()
    take(across)

    for index in (3, 4, 5):
        loads[index].wait()

    @pl.loop(1, 8)
    def _(j):
        src = lax.rem(s + 8 - j, NS)
        remote(
            att_row.at[cols(src), :], att_tok.at[:, cols(src)], a1_ss.at[src], a1_rs.at[src], (g, src, d)
        ).wait_recv()

    big[...] = mm_nt(att_tok[...], wo[...])
    gate_row = mod[2]

    @pl.loop(0, TOK // 16, unroll=4)
    def _(i):
        rows = pl.ds(pl.multiple_of(i * 16, 16), 16)
        mixed = hid[rows, :].astype(F32) + gate_row * big[rows, :]
        y, r = norm_rows(mixed)
        fin[rows, :] = y
        rstd[rows, :] = jnp.broadcast_to(r, (16, 128))
        tokbf[rows, :] = y.astype(BF16)

    step = jnp.full((TOK, 64), steps[0], jnp.int32).astype(F32)
    angle = (step / 1000 + 0.008) / 1.008 * (math.pi / 2)
    target = jnp.cos(angle) * noise[...].T - jnp.sin(angle) * ltok[:, 0:64]
    pred_grad = ((2.0 / 64) * (mm_nt(tokbf[...], wp[...]) - target)).astype(BF16)
    big[...] = mm(pred_grad, wp[...])

    @pl.loop(0, TOK // 16, unroll=4)
    def _(i):
        rows = pl.ds(pl.multiple_of(i * 16, 16), 16)
        dy = big[rows, :]
        y = fin[rows, :]
        mean_dy = jnp.mean(dy, axis=-1, keepdims=True)
        mean_dyy = jnp.mean(dy * y, axis=-1, keepdims=True)
        dx = (dy - mean_dy - y * mean_dyy) * rstd[rows, 0:1]
        tokbf[rows, :] = (gate_row * dx).astype(BF16)

    ag_tok[...] = mm(tokbf[...], wo[...]).astype(BF16)

    def ag_copy(j):
        peer = lax.rem(s + j, NS)
        return remote(
            ag_tok.at[:, cols(peer)], ag_head.at[cols(s), :], a2_ss.at[j], a2_rs.at[s], (g, peer, d)
        )

    @pl.loop(1, 8)
    def _(j):
        ag_copy(j).start()

    ag_head[cols(s), :] = ag_tok[:, cols(s)]
    @pl.loop(1, 8)
    def _(j):
        src = lax.rem(s + 8 - j, NS)
        remote(
            ag_tok.at[:, cols(src)], ag_head.at[cols(src), :], a2_ss.at[j], a2_rs.at[src], (g, src, d)
        ).wait_recv()

    @pl.loop(0, 8)
    def _(j):
        here = cols(j)
        val = ag_head[here, :].astype(F32).T
        agT[:, here] = val.astype(BF16)
        num[:, here] = val * attT[:, here].astype(F32)

    def v_copy(c):
        rows = cols(c, KB)
        return remote(
            igv.at[rows, :], igv_sib.at[rows, :], sv_ss.at[c], sv_rs.at[c], (1 - g, s, d)
        )

    low_k = lax.broadcasted_iota(jnp.int32, (KB, 128), 1) < 64

    @pl.loop(0, S // KB)
    def _(c):
        rows = cols(c, KB)
        dvs = []
        for h in range(2):
            p = eT[h, rows, :] * invs[h : h + 1, :]
            dvs.append(mm(p.astype(BF16), ag_head[...]))
        igv[rows, :] = jnp.where(low_k, dvs[0], dvs[1]).astype(BF16)
        v_copy(c).start()

    deltas = [jnp.sum(num[h * 64 : h * 64 + 64, :], axis=0, keepdims=True) for h in range(2)]
    dqT[...] = jnp.zeros_like(dqT)

    def score_back(c):
        rows = cols(c, KB)
        dks = []
        for h in range(2):
            p = eT[h, rows, :] * invs[h : h + 1, :]
            dp = mm(vmask[h, rows, :], agT[...])
            ds = (p * (dp - deltas[h])).astype(BF16)
            dks.append(mm(ds, qrow[...]))
            hr = slice(h * 64, h * 64 + 64)
            dqT[hr, :] += mm(kT[hr, rows], ds)
        dk[rows, :] = jnp.where(low_k, dks[0], dks[1]) * 0.125

    @pl.loop(0, 2)
    def _(c):
        score_back(c)

    def grad_rows(i, mine, theirs):
        rows = pl.ds(pl.multiple_of(g * HALF + i * 240, 16), 240)
        value = mm(nT[rows, :], mine[...])
        return value + mm(nT_sib[pl.ds(pl.multiple_of(i * 240, 16), 240), :], theirs[...])

    def dpv_copy(c):
        return remote(wgv.at[c], dpv.at[d], dv_ss.at[c], dv_rs.at[d], (g, s, c))

    def dpq_copy(c):
        return remote(wgq.at[c], dpq.at[d], dq_ss.at[c], dq_rs.at[d], (g, s, c))

    arrived(over_down, 1)
    arrived(over_up, 0)
    arrived(over_two, 0)
    arrived(over_two, 1)

    @pl.loop(0, 3)
    def _(j):
        take(jnp.where(j == 0, over_down, jnp.where(j == 1, over_up, over_two)))

    @pl.loop(0, 8)
    def _(j):
        norm_copy(j).wait_recv()

    @pl.loop(0, S // KB)
    def _(c):
        v_copy(c).wait_recv()

    @pl.loop(0, 4)
    def _(j):
        i = lax.rem(d // 2 + 1 + j, 4)
        value = grad_rows(i, igv, igv_sib)
        for q in range(2):
            c = 2 * i + q
            wgv[c] = value[q * PART : q * PART + PART]

            @pl.when(c != d)
            def _():
                dpv_copy(c).start()

    @pl.loop(2, 4)
    def _(c):
        score_back(c)

    inv_gq = 1.0 / gq
    inv_gk = 1.0 / gk

    def ig_copy(j):
        here = cols(j)
        return remote(
            ig.at[here, :], ig_sib.at[here, :], sb_ss.at[j], sb_rs.at[j], (1 - g, s, d)
        )

    @pl.loop(0, 8)
    def _(j):
        here = cols(j)
        xhat = qT[:, here].astype(F32) * inv_gq
        grad = head_norm_back_t(dqT[:, here] * 0.125 * gq, xhat, r_all[j, 0:2, :])
        ig[here, 0:128] = grad.T.astype(BF16)
        xhat = kT[:, here].astype(F32) * inv_gk
        grad = head_norm_back_t(dk[here, :].T * gk, xhat, r_all[j, 2:4, :])
        ig[here, 128:256] = grad.T.astype(BF16)
        ig_copy(j).start()

    @pl.loop(0, 8)
    def _(j):
        ig_copy(j).wait_recv()

    @pl.loop(0, 4)
    def _(j):
        i = lax.rem(d // 2 + 1 + j, 4)
        value = grad_rows(i, ig, ig_sib)
        for q in range(2):
            c = 2 * i + q
            wgq[c] = value[q * PART : q * PART + PART]

            @pl.when(c != d)
            def _():
                dpq_copy(c).start()

    def finish_columns(own, arrived, part_sem, total, out_send, out_recv, send_sem, recv_sem):
        total[PART:, :] = jnp.zeros((128 - PART, total.shape[1]), F32)
        total[0:PART, :] = own[d]

        @pl.loop(1, 8)
        def _(j):
            src = lax.rem(d + 8 - j, ND)
            remote(own.at[src], arrived.at[src], part_sem.at[src], part_sem.at[src], (g, s, src)).wait_recv()
            total[0:PART, :] += arrived[src]

        for j in range(8):
            out_send[j] = total[j * OUT_ROWS : j * OUT_ROWS + 16, :]

        @pl.loop(0, 8)
        def _(j):
            me = jnp.logical_and(s == d, j == d)

            @pl.when(me)
            def _():
                out_recv[s] = out_send[j]

            @pl.when(jnp.logical_not(me))
            def _():
                remote(
                    out_send.at[j], out_recv.at[s], send_sem.at[j], recv_sem.at[s], (g, d, j)
                ).start()

    finish_columns(wgv, dpv, dv_rs, accv, fsv, frv, fv_ss, fv_rs)
    finish_columns(wgq, dpq, dq_rs, accq, fsq, frq, fq_ss, fq_rs)

    @pl.loop(0, 8)
    def _(j):
        me = jnp.logical_and(s == d, j == d)

        @pl.when(jnp.logical_not(me))
        def _():
            remote(fsv.at[j], frv.at[j], fv_ss.at[j], fv_rs.at[j], (g, j, s)).wait_recv()
            remote(fsq.at[j], frq.at[j], fq_ss.at[j], fq_rs.at[j], (g, j, s)).wait_recv()

    for j in range(8):
        lanes = slice(j * 128, j * 128 + 128)
        out_ref[:, lanes] = frq[j, 0:OUT_ROWS, 0:128]
        out_ref[:, INNER + j * 128 : INNER + j * 128 + 128] = frq[j, 0:OUT_ROWS, 128:256]
        out_ref[:, 2 * INNER + j * 128 : 2 * INNER + j * 128 + 128] = frv[j, 0:OUT_ROWS, :]

    for copy in own_sends:
        copy.wait_send()

    @pl.loop(6, 14)
    def _(sem):
        pass_on(0, 0, sem, z_up).wait_send()

    @pl.loop(1, 8)
    def _(j):
        att_copy(lax.rem(s + j, NS)).wait_send()
        ag_copy(j).wait_send()

    @pl.loop(0, 8)
    def _(j):
        ig_copy(j).wait_send()
        norm_copy(j).wait_send()

    @pl.loop(0, 4)
    def _(j):
        qkv_copy(j, 0).wait_send()
        r_copy(j, 0).wait_send()

    @pl.loop(0, S // KB)
    def _(c):
        v_copy(c).wait_send()

    @pl.loop(1, 16)
    def _(j):
        latent_copy(j).wait_send()


    @pl.loop(0, 8)
    def _(c):
        @pl.when(c != d)
        def _():
            dpv_copy(c).wait_send()
            dpq_copy(c).wait_send()

        me = jnp.logical_and(s == d, c == d)

        @pl.when(jnp.logical_not(me))
        def _():
            remote(fsv.at[c], frv.at[s], fv_ss.at[c], fv_rs.at[s], (g, d, c)).wait_send()
            remote(fsq.at[c], frq.at[s], fq_ss.at[c], fq_rs.at[s], (g, d, c)).wait_send()


def scratch_shapes():
    V = pltpu.VMEM
    dma = pltpu.SemaphoreType.DMA
    return [
        V((512, C), BF16),
        V((432, C), BF16),
        V((TOK, D), BF16),
        V((64, TOK), F32),
        V((D, 2 * W3), BF16),
        V((D, INNER), BF16),
        V((64, D), BF16),
        V((NS, TOK, D), BF16),
        V((D, S), BF16),
        V((2 * W3, D), BF16),
        V((4, W3, TOK), BF16),
        V((W3, S), BF16),
        V((4, 8, TOK), F32),
        V((NS, 8, TOK), F32),
        V((512, W3), F32),
        V((16, 32, 128), F32),
        V((16, 32, 128), F32),
        V((512, 128), F32),
        V((TOK, 128), F32),
        V((S, 128), BF16),
        V((2, S, 128), BF16),
        V((2, S, 128), BF16),
        V((2, S, S), F32),
        V((128, S), F32),
        V((128, S), BF16),
        V((S, 128), BF16),
        V((TOK, INNER), BF16),
        V((TOK, D), F32),
        V((TOK, D), F32),
        V((TOK, 128), F32),
        V((TOK, D), BF16),
        V((TOK, INNER), BF16),
        V((S, 128), BF16),
        V((128, S), BF16),
        V((128, S), F32),
        V((S, 128), F32),
        V((S, 256), BF16),
        V((S, 256), BF16),
        V((S, 128), BF16),
        V((S, 128), BF16),
        V((HALF, S), BF16),
        V((2, S), F32),
        V((8, PART, 128), F32),
        V((8, PART, 256), F32),
        V((8, PART, 128), F32),
        V((8, PART, 256), F32),
        V((128, 128), F32),
        V((128, 256), F32),
        V((8, 16, 128), F32),
        V((8, 16, 256), F32),
        V((8, 16, 128), F32),
        V((8, 16, 256), F32),
        dma((6,)),
        dma((14,)),
        dma((16,)),
        dma((16,)),
        dma((16,)),
        dma((8,)),
        dma((8,)),
        dma((8,)),
        dma((8,)),
        dma((8,)),
        dma((8,)),
        dma((4,)),
        dma((4,)),
        dma((8,)),
        dma((8,)),
        dma((8,)),
        dma((8,)),
        dma((8,)),
        dma((8,)),
        dma((8,)),
        dma((8,)),
        dma((8,)),
        dma((8,)),
        dma((6,)),
        dma((8,)),
        dma((8,)),
        dma((8,)),
        dma((8,)),
    ]


def local(
    features,
    group_gain,
    group_bias,
    conv_weight,
    hidden,
    modulation,
    timesteps,
    fresh_noise,
    input_weight,
    query_gain,
    key_gain,
    output_weight,
    patch_weight,
):
    vmem = pl.BlockSpec(memory_space=pltpu.VMEM)
    hbm = pl.BlockSpec(memory_space=pl.ANY)
    return pl.pallas_call(
        kernel,
        out_shape=jax.ShapeDtypeStruct((OUT_ROWS, 3 * INNER), F32),
        in_specs=[pl.BlockSpec(memory_space=pltpu.SMEM)] + [vmem] * 5 + [hbm] * 7,
        out_specs=vmem,
        scratch_shapes=scratch_shapes(),
        compiler_params=pltpu.CompilerParams(
            collective_id=0, has_side_effects=True, vmem_limit_bytes=60 * 2**20
        ),
    )(
        timesteps.reshape(1),
        group_gain.reshape(1, C),
        group_bias.reshape(1, C),
        modulation.reshape(3, 1, D),
        query_gain.reshape(1, 64),
        key_gain.reshape(1, 64),
        features.reshape(512, C),
        conv_weight.T,
        hidden.reshape(TOK, D),
        fresh_noise.reshape(TOK, 64).T,
        input_weight,
        output_weight,
        patch_weight.T,
    )


def solution(mesh):
    in_specs = (
        P("dp", None, None, ("grp", "seq"), None, None),
        P(),
        P(),
        P(),
        P("grp", None, "dp", "seq", None),
        P("grp", None, "dp", None, None),
        P("grp", None, "dp"),
        P("grp", None, "dp", "seq", None),
        P(),
        P(),
        P(),
        P(),
        P(),
    )
    out_specs = P(("grp", "seq", "dp"), None)
    return jax.shard_map(local, mesh=mesh, in_specs=in_specs, out_specs=out_specs, check_vma=False)
```

```python
import math

import jax
import jax.numpy as jnp
from jax import lax
from jax.experimental import pallas as pl
from jax.experimental.pallas import tpu as pltpu
from jax.sharding import PartitionSpec as P

F32 = jnp.float32
BF16 = jnp.bfloat16
MESH = pl.DeviceIdType.MESH

NG, NS, ND = 2, 8, 8
D = 1920
INNER = 1024
S = 1024
TOK = 128
W3 = 384
C = 512
HALF = D // NG
PART = HALF // ND
OUT_ROWS = 15
KB = 256
LATENT_SCALE = 1.15258426
GROUP_EPS = 1e-06
LAYER_EPS = 1e-05
HEAD_EPS = 1e-06


def mm(a, b):
    return lax.dot_general(a, b, (((1,), (0,)), ((), ())), preferred_element_type=F32)


def mm_nt(a, b):
    return lax.dot_general(a, b, (((1,), (1,)), ((), ())), preferred_element_type=F32)


def norm_rows(x):
    mu = jnp.mean(x, axis=-1, keepdims=True)
    centred = x - mu
    var = jnp.mean(centred * centred, axis=-1, keepdims=True)
    r = lax.rsqrt(var + LAYER_EPS)
    return centred * r, r


def head_norm_t(x):
    x3 = x.reshape(2, 64, x.shape[1])
    mu = jnp.mean(x3, axis=1, keepdims=True)
    centred = x3 - mu
    var = jnp.mean(centred * centred, axis=1, keepdims=True)
    r = lax.rsqrt(var + HEAD_EPS)
    return (centred * r).reshape(x.shape), r[:, 0, :]


def head_norm_back_t(grad, xhat, r):
    g3 = grad.reshape(2, 64, grad.shape[1])
    x3 = xhat.reshape(2, 64, grad.shape[1])
    mean_g = jnp.mean(g3, axis=1, keepdims=True)
    mean_gx = jnp.mean(g3 * x3, axis=1, keepdims=True)
    return ((g3 - mean_g - x3 * mean_gx) * r[:, None, :]).reshape(grad.shape)


def gain_columns(gain_row):
    both = jnp.concatenate([gain_row, gain_row], axis=1)
    return jnp.broadcast_to(both, (128, 128)).T


def group_mean(v, count):
    lane = lax.broadcasted_iota(jnp.int32, v.shape, 1)
    for step in (1, 2, 4, 8):
        up = pltpu.roll(v, C - step, 1)
        down = pltpu.roll(v, step, 1)
        v = v + jnp.where((lane & step) == 0, up, down)
    return v * (1.0 / count)


def kernel(
    steps,
    ggain,
    gbias,
    mod,
    qgain,
    kgain,
    feat_hbm,
    cw_hbm,
    hid_hbm,
    noise_hbm,
    w_hbm,
    wo_hbm,
    wp_hbm,
    out_ref,
    feat,
    cw,
    hid,
    noise,
    wq,
    wo,
    wp,
    ng,
    nT,
    wqT,
    qkv_send,
    qkvT,
    r_send,
    r_all,
    taps,
    vsend,
    vrecv,
    lat,
    ltok,
    qrow,
    kmask,
    vmask,
    eT,
    num,
    attT,
    att_row,
    att_tok,
    big,
    fin,
    rstd,
    tokbf,
    ag_tok,
    ag_head,
    agT,
    dqT,
    dk,
    ig,
    ig_sib,
    igv,
    igv_sib,
    nT_sib,
    invs,
    wgv,
    wgq,
    dpv,
    dpq,
    accv,
    accq,
    fsv,
    fsq,
    frv,
    frq,
    ld_sem,
    ag_ss,
    ag_rs,
    lt_ss,
    lt_rs,
    a1_ss,
    a1_rs,
    a2_ss,
    a2_rs,
    sb_ss,
    sb_rs,
    sv_ss,
    sv_rs,
    dv_ss,
    dv_rs,
    dq_ss,
    dq_rs,
    fv_ss,
    fv_rs,
    fq_ss,
    fq_rs,
    nt_ss,
    nt_rs,
    w_sem,
    q_ss,
    q_rs,
    r_ss,
    r_rs,
):
    g = lax.axis_index("grp")
    s = lax.axis_index("seq")
    d = lax.axis_index("dp")
    tile = g * NS + s

    def remote(src, dst, ssem, rsem, dev):
        return pltpu.make_async_remote_copy(
            src_ref=src, dst_ref=dst, send_sem=ssem, recv_sem=rsem, device_id=dev, device_id_type=MESH
        )

    def cols(index, width=128):
        return pl.ds(pl.multiple_of(index * width, width), width)

    yh, z = s // 4, lax.rem(s, 4)
    over = (1 - yh) * 4
    across = over + z
    w_loads = [
        pltpu.make_async_copy(
            w_hbm.at[:, cols(owner + 8 * part)],
            wq.at[:, who * W3 + part * 128 : who * W3 + part * 128 + 128],
            w_sem.at[who * 3 + part],
        )
        for who, owner in enumerate((s, across))
        for part in range(3)
    ]
    hid_load = pltpu.make_async_copy(hid_hbm, hid, ld_sem.at[0])
    hid_load.start()
    for copy in w_loads:
        copy.start()

    loads = [
        hid_load,
        pltpu.make_async_copy(feat_hbm, feat, ld_sem.at[1]),
        pltpu.make_async_copy(cw_hbm, cw, ld_sem.at[2]),
        pltpu.make_async_copy(noise_hbm, noise, ld_sem.at[3]),
        pltpu.make_async_copy(wo_hbm, wo, ld_sem.at[4]),
        pltpu.make_async_copy(wp_hbm, wp, ld_sem.at[5]),
    ]
    for copy in loads[1:]:
        copy.start()

    barrier = pltpu.get_barrier_semaphore()

    def greet(dev):
        pl.semaphore_signal(barrier, inc=1, device_id=dev, device_id_type=MESH)

    @pl.loop(1, 16)
    def _(j):
        t = lax.rem(tile + j, 16)
        greet((t // NS, lax.rem(t, NS), d))

    @pl.loop(1, 8)
    def _(j):
        greet((g, s, lax.rem(d + j, ND)))

    @pl.loop(0, 8)
    def _(j):
        me = jnp.logical_and(s == d, j == d)

        @pl.when(jnp.logical_not(me))
        def _():
            greet((g, d, j))
            greet((g, j, s))

    loads[0].wait()
    shift_row = mod[0]
    scale_row = 1.0 + mod[1]

    @pl.loop(0, TOK // 16, unroll=4)
    def _(i):
        rows = pl.ds(pl.multiple_of(i * 16, 16), 16)
        y, _ = norm_rows(hid[rows, :].astype(F32))
        ng[s, rows, :] = (y * scale_row + shift_row).astype(BF16)

    selfs = jnp.where(s == d, 2, 0)
    pl.semaphore_wait(barrier, 15 + 7 + 16 - selfs)

    z_up = yh * 4 + lax.rem(z + 1, 4)
    z_down = yh * 4 + lax.rem(z + 3, 4)

    def pass_on(slot, half, sem, peer):
        block = ng.at[slot, pl.ds(half * 64, 64), :]
        return remote(block, block, ag_ss.at[sem], ag_rs.at[slot * 2 + half], (g, peer, d))

    def arrived(slot, half):
        pass_on(slot, half, 0, z_up).wait_recv()

    z_two = yh * 4 + lax.rem(z + 2, 4)
    over_up = over + lax.rem(z + 1, 4)
    over_down = over + lax.rem(z + 3, 4)
    over_two = over + lax.rem(z + 2, 4)
    own_sends = [
        pass_on(s, 0, 0, z_up),
        pass_on(s, 1, 1, z_down),
        pass_on(s, 0, 2, across),
        pass_on(s, 1, 3, z_up),
        pass_on(s, 0, 4, z_down),
        pass_on(s, 1, 5, across),
    ]
    for copy in own_sends:
        copy.start()

    loads[1].wait()
    loads[2].wait()
    row_id = lax.broadcasted_iota(jnp.int32, (W3, 432), 1)
    col_id = lax.broadcasted_iota(jnp.int32, (W3, 432), 0)
    inner = col_id & 127
    src0 = (col_id >> 7) * 144 + (inner >> 4) * 48 + (inner & 15)
    used = inner < 48
    cw_val = cw[...]
    col_w = lax.broadcasted_iota(jnp.int32, (C, C), 0) & 15
    acts = []
    for clip in range(2):
        x = feat[clip * 256 : clip * 256 + 256, :].astype(F32)
        mean = group_mean(jnp.broadcast_to(jnp.sum(x, axis=0, keepdims=True), (8, C)), 4096.0)[0:1]
        centred = x - mean
        var = group_mean(
            jnp.broadcast_to(jnp.sum(centred * centred, axis=0, keepdims=True), (8, C)), 4096.0
        )[0:1]
        normed = centred * lax.rsqrt(var + GROUP_EPS) * ggain[...] + gbias[...]
        acts.append(normed / (1.0 + jnp.exp(-normed)))
    act = jnp.concatenate(acts, axis=0)
    for e in range(3):
        pick = jnp.where(jnp.logical_and(used, row_id == src0 + e * 16), 1.0, 0.0).astype(BF16)
        we = mm(pick, cw_val).astype(BF16)
        if e == 0:
            ae = jnp.where(col_w == 0, 0.0, pltpu.roll(act, 1, 0))
        elif e == 2:
            ae = jnp.where(col_w == 15, 0.0, pltpu.roll(act, C - 1, 0))
        else:
            ae = act
        term = mm_nt(ae.astype(BF16), we)
        if e == 0:
            taps[...] = term
        else:
            taps[...] += term
    for clip in range(2):
        for frame in range(8):
            total = None
            for a in range(3):
                base = (clip * 8 + max(frame + a - 2, 0)) * 32
                piece = taps[base : base + 32, a * 128 : a * 128 + 128]
                total = piece if total is None else total + piece
            vsend[clip * 8 + frame] = total
    vrecv[tile] = vsend[tile]

    def latent_copy(j):
        t = lax.rem(tile + j, 16)
        return remote(
            vsend.at[t], vrecv.at[tile], lt_ss.at[j], lt_rs.at[tile], (t // NS, lax.rem(t, NS), d)
        )

    def norm_copy(slot):
        return remote(
            nT.at[pl.ds(pl.multiple_of((1 - g) * HALF, 16), HALF), cols(slot)],
            nT_sib.at[:, cols(slot)],
            nt_ss.at[slot],
            nt_rs.at[slot],
            (1 - g, s, d),
        )

    def take(slot):
        nT[:, cols(slot)] = ng[slot].T
        norm_copy(slot).start()

    for copy in w_loads:
        copy.wait()

    @pl.loop(0, 15)
    def _(i):
        wqT[:, cols(i)] = wq[cols(i), :].T

    gq = gain_columns(qgain[...])
    gk = gain_columns(kgain[...])
    low = lax.broadcasted_iota(jnp.int32, (128, 128), 1) < 64
    r_send[...] = jnp.zeros_like(r_send)

    def hop(j):
        step = jnp.where(j == 1, 3, jnp.where(j == 2, 1, jnp.where(j == 3, 2, 0)))
        return lax.rem(z + step, 4)

    def qkv_copy(j, src):
        return remote(
            qkv_send.at[j], qkvT.at[:, cols(src)], q_ss.at[j], q_rs.at[src], (g, across, d)
        )

    def r_copy(j, src):
        return remote(r_send.at[j], r_all.at[src], r_ss.at[j], r_rs.at[src], (g, across, d))

    def rows_of(here, query, key, value):
        qrow[here, :] = query.T.astype(BF16)
        row = key.T
        kmask[0, here, :] = jnp.where(low, row, 0.0).astype(BF16)
        kmask[1, here, :] = jnp.where(low, 0.0, row).astype(BF16)
        row = value.T
        vmask[0, here, :] = jnp.where(low, row, 0.0).astype(BF16)
        vmask[1, here, :] = jnp.where(low, 0.0, row).astype(BF16)

    @pl.loop(0, 4)
    def _(j):
        src = yh * 4 + hop(j)

        @pl.when(j == 1)
        def _():
            arrived(z_down, 0)
            pass_on(z_down, 0, 6, z_up).start()
            arrived(z_up, 1)
            pass_on(z_up, 1, 7, z_down).start()
            arrived(z_down, 1)

        @pl.when(j == 2)
        def _():
            arrived(z_up, 0)
            for half in range(2):
                arrived(across, half)
                pass_on(across, half, 8 + 2 * half, z_up).start()
                pass_on(across, half, 9 + 2 * half, z_down).start()

        @pl.when(j == 3)
        def _():
            arrived(z_two, 0)
            arrived(z_two, 1)

        here = cols(src)
        take(src)
        pT = mm(wqT[...], nT[:, here])
        for who in (1, 0):
            base = who * W3
            query, rq = head_norm_t(pT[base : base + 128])
            key, rk = head_norm_t(pT[base + 128 : base + 256])
            query = query * gq
            key = key * gk
            value = pT[base + 256 : base + 384]
            if who == 1:
                qkv_send[j, 0:128, :] = query.astype(BF16)
                qkv_send[j, 128:256, :] = key.astype(BF16)
                qkv_send[j, 256:384, :] = value.astype(BF16)
                r_send[j, 0:2, :] = rq
                r_send[j, 2:4, :] = rk
                qkv_copy(j, src).start()
                r_copy(j, src).start()
            else:
                qkvT[0:128, here] = query.astype(BF16)
                qkvT[128:256, here] = key.astype(BF16)
                qkvT[256:384, here] = value.astype(BF16)
                r_all[src] = jnp.zeros((8, TOK), F32)
                r_all[src, 0:2, :] = rq
                r_all[src, 2:4, :] = rk
                rows_of(here, query, key, value)

    @pl.loop(1, 16)
    def _(j):
        latent_copy(j).start()

    @pl.loop(0, 4)
    def _(j):
        src = over + hop(j)
        qkv_copy(j, src).wait_recv()
        r_copy(j, src).wait_recv()
        here = cols(src)
        rows_of(
            here,
            qkvT[0:128, here].astype(F32),
            qkvT[128:256, here].astype(F32),
            qkvT[256:384, here].astype(F32),
        )

    qT = qkvT.at[0:128]
    kT = qkvT.at[128:256]
    vT = qkvT.at[256:384]

    def att_copy(peer):
        return remote(
            att_row.at[cols(peer), :],
            att_tok.at[:, cols(s)],
            a1_ss.at[peer],
            a1_rs.at[s],
            (g, peer, d),
        )

    @pl.loop(0, S // KB)
    def _(j):
        c = lax.rem(s // 2 + 1 + j, S // KB)
        here = cols(c, KB)
        for h in range(2):
            hr = slice(h * 64, h * 64 + 64)
            e = jnp.exp(mm(kmask[h], qT[:, here]) * 0.125)
            eT[h, :, here] = e
            inv = 1.0 / jnp.sum(e, axis=0, keepdims=True)
            invs[h : h + 1, here] = inv
            num[hr, here] = mm(vT[hr, :], e.astype(BF16)) * inv
        val = num[:, here]
        attT[:, here] = val.astype(BF16)
        att_row[here, :] = val.T.astype(BF16)
        for q in range(2):
            peer = 2 * c + q

            @pl.when(peer != s)
            def _():
                att_copy(peer).start()

    att_tok[:, cols(s)] = att_row[cols(s), :]

    @pl.loop(1, 16)
    def _(j):
        t = lax.rem(tile + j, 16)
        remote(
            vsend.at[t], vrecv.at[t], lt_ss.at[j], lt_rs.at[t], (t // NS, lax.rem(t, NS), d)
        ).wait_recv()

    x = vrecv[...].reshape(512, 128)
    pad = jnp.zeros((16, 128), F32)
    total = jnp.concatenate([pad, x[:-16]], axis=0) + pltpu.roll(x, 112, 1)
    total = total + jnp.concatenate([pltpu.roll(x, 96, 1)[16:], pad], axis=0)
    lane = lax.broadcasted_iota(jnp.int32, (512, 128), 1)
    lat[...] = jnp.where(lane < 16, total * LATENT_SCALE, 0.0)
    tokens = jnp.zeros((128, 128), F32)
    for jj in range(2):
        half = lat[pl.ds(jj, 256, stride=2), :].reshape(16, 2, 8, 128)
        for ii in range(2):
            piece = half[:, ii].reshape(128, 128)
            place = 16 * (2 * ii + jj)
            tokens = tokens + (pltpu.roll(piece, place, 1) if place else piece)
    ltok[...] = tokens

    arrived(over_down, 0)
    pass_on(over_down, 0, 12, z_up).start()
    arrived(over_up, 1)
    pass_on(over_up, 1, 13, z_down).start()
    take(across)

    for index in (3, 4, 5):
        loads[index].wait()

    @pl.loop(1, 8)
    def _(j):
        src = lax.rem(s + 8 - j, NS)
        remote(
            att_row.at[cols(src), :], att_tok.at[:, cols(src)], a1_ss.at[src], a1_rs.at[src], (g, src, d)
        ).wait_recv()

    big[...] = mm_nt(att_tok[...], wo[...])
    gate_row = mod[2]

    @pl.loop(0, TOK // 16, unroll=4)
    def _(i):
        rows = pl.ds(pl.multiple_of(i * 16, 16), 16)
        mixed = hid[rows, :].astype(F32) + gate_row * big[rows, :]
        y, r = norm_rows(mixed)
        fin[rows, :] = y
        rstd[rows, :] = jnp.broadcast_to(r, (16, 128))
        tokbf[rows, :] = y.astype(BF16)

    step = jnp.full((TOK, 64), steps[0], jnp.int32).astype(F32)
    angle = (step / 1000 + 0.008) / 1.008 * (math.pi / 2)
    target = jnp.cos(angle) * noise[...].T - jnp.sin(angle) * ltok[:, 0:64]
    pred_grad = ((2.0 / 64) * (mm_nt(tokbf[...], wp[...]) - target)).astype(BF16)
    big[...] = mm(pred_grad, wp[...])

    @pl.loop(0, TOK // 16, unroll=4)
    def _(i):
        rows = pl.ds(pl.multiple_of(i * 16, 16), 16)
        dy = big[rows, :]
        y = fin[rows, :]
        mean_dy = jnp.mean(dy, axis=-1, keepdims=True)
        mean_dyy = jnp.mean(dy * y, axis=-1, keepdims=True)
        dx = (dy - mean_dy - y * mean_dyy) * rstd[rows, 0:1]
        tokbf[rows, :] = (gate_row * dx).astype(BF16)

    ag_tok[...] = mm(tokbf[...], wo[...]).astype(BF16)

    def ag_copy(j):
        peer = lax.rem(s + j, NS)
        return remote(
            ag_tok.at[:, cols(peer)], ag_head.at[cols(s), :], a2_ss.at[j], a2_rs.at[s], (g, peer, d)
        )

    @pl.loop(1, 8)
    def _(j):
        ag_copy(j).start()

    ag_head[cols(s), :] = ag_tok[:, cols(s)]
    @pl.loop(1, 8)
    def _(j):
        src = lax.rem(s + 8 - j, NS)
        remote(
            ag_tok.at[:, cols(src)], ag_head.at[cols(src), :], a2_ss.at[j], a2_rs.at[src], (g, src, d)
        ).wait_recv()

    @pl.loop(0, 8)
    def _(j):
        here = cols(j)
        val = ag_head[here, :].astype(F32).T
        agT[:, here] = val.astype(BF16)
        num[:, here] = val * attT[:, here].astype(F32)

    def v_copy(c):
        rows = cols(c, KB)
        return remote(
            igv.at[rows, :], igv_sib.at[rows, :], sv_ss.at[c], sv_rs.at[c], (1 - g, s, d)
        )

    low_k = lax.broadcasted_iota(jnp.int32, (KB, 128), 1) < 64

    @pl.loop(0, S // KB)
    def _(c):
        rows = cols(c, KB)
        dvs = []
        for h in range(2):
            p = eT[h, rows, :] * invs[h : h + 1, :]
            dvs.append(mm(p.astype(BF16), ag_head[...]))
        igv[rows, :] = jnp.where(low_k, dvs[0], dvs[1]).astype(BF16)
        v_copy(c).start()

    deltas = [jnp.sum(num[h * 64 : h * 64 + 64, :], axis=0, keepdims=True) for h in range(2)]
    dqT[...] = jnp.zeros_like(dqT)

    def score_back(c):
        rows = cols(c, KB)
        dks = []
        for h in range(2):
            p = eT[h, rows, :] * invs[h : h + 1, :]
            dp = mm(vmask[h, rows, :], agT[...])
            ds = (p * (dp - deltas[h])).astype(BF16)
            dks.append(mm(ds, qrow[...]))
            hr = slice(h * 64, h * 64 + 64)
            dqT[hr, :] += mm(kT[hr, rows], ds)
        dk[rows, :] = jnp.where(low_k, dks[0], dks[1]) * 0.125

    @pl.loop(0, 2)
    def _(c):
        score_back(c)

    def grad_rows(i, mine, theirs):
        rows = pl.ds(pl.multiple_of(g * HALF + i * 240, 16), 240)
        value = mm(nT[rows, :], mine[...])
        return value + mm(nT_sib[pl.ds(pl.multiple_of(i * 240, 16), 240), :], theirs[...])

    def padded(value, q):
        blank = jnp.zeros((128 - PART, value.shape[1]), F32)
        return jnp.concatenate([value[q * PART : q * PART + PART], blank], axis=0)

    def dpv_copy(c):
        return remote(wgv.at[c], dpv.at[d], dv_ss.at[c], dv_rs.at[d], (g, s, c))

    def dpq_copy(c):
        return remote(wgq.at[c], dpq.at[d], dq_ss.at[c], dq_rs.at[d], (g, s, c))

    arrived(over_down, 1)
    arrived(over_up, 0)
    arrived(over_two, 0)
    arrived(over_two, 1)

    @pl.loop(0, 3)
    def _(j):
        take(jnp.where(j == 0, over_down, jnp.where(j == 1, over_up, over_two)))

    @pl.loop(0, 8)
    def _(j):
        norm_copy(j).wait_recv()

    @pl.loop(0, S // KB)
    def _(c):
        v_copy(c).wait_recv()

    @pl.loop(0, 4)
    def _(j):
        i = lax.rem(d // 2 + 1 + j, 4)
        value = grad_rows(i, igv, igv_sib)
        for q in range(2):
            c = 2 * i + q
            part = padded(value, q)

            @pl.when(c == d)
            def _():
                accv[...] = part

            @pl.when(c != d)
            def _():
                wgv[c] = part[0:PART]
                dpv_copy(c).start()

    @pl.loop(2, 4)
    def _(c):
        score_back(c)

    inv_gq = 1.0 / gq
    inv_gk = 1.0 / gk

    def ig_copy(j):
        here = cols(j)
        return remote(
            ig.at[here, :], ig_sib.at[here, :], sb_ss.at[j], sb_rs.at[j], (1 - g, s, d)
        )

    @pl.loop(0, 8)
    def _(j):
        here = cols(j)
        xhat = qT[:, here].astype(F32) * inv_gq
        grad = head_norm_back_t(dqT[:, here] * 0.125 * gq, xhat, r_all[j, 0:2, :])
        ig[here, 0:128] = grad.T.astype(BF16)
        xhat = kT[:, here].astype(F32) * inv_gk
        grad = head_norm_back_t(dk[here, :].T * gk, xhat, r_all[j, 2:4, :])
        ig[here, 128:256] = grad.T.astype(BF16)
        ig_copy(j).start()

    @pl.loop(0, 8)
    def _(j):
        ig_copy(j).wait_recv()

    @pl.loop(0, 4)
    def _(j):
        i = lax.rem(d // 2 + 1 + j, 4)
        value = grad_rows(i, ig, ig_sib)
        for q in range(2):
            c = 2 * i + q
            part = padded(value, q)

            @pl.when(c == d)
            def _():
                accq[...] = part

            @pl.when(c != d)
            def _():
                wgq[c] = part.astype(BF16)
                dpq_copy(c).start()

    def finish_columns(own, arrived, part_sem, total, out_send, out_recv, send_sem, recv_sem):
        @pl.loop(1, 8)
        def _(j):
            src = lax.rem(d + 8 - j, ND)
            remote(own.at[src], arrived.at[src], part_sem.at[src], part_sem.at[src], (g, s, src)).wait_recv()
            total[0 : arrived.shape[1], :] += arrived[src].astype(F32)

        for j in range(8):
            out_send[j] = total[j * OUT_ROWS : j * OUT_ROWS + 16, :]

        @pl.loop(0, 8)
        def _(j):
            me = jnp.logical_and(s == d, j == d)

            @pl.when(me)
            def _():
                out_recv[s] = out_send[j]

            @pl.when(jnp.logical_not(me))
            def _():
                remote(
                    out_send.at[j], out_recv.at[s], send_sem.at[j], recv_sem.at[s], (g, d, j)
                ).start()

    finish_columns(wgv, dpv, dv_rs, accv, fsv, frv, fv_ss, fv_rs)
    finish_columns(wgq, dpq, dq_rs, accq, fsq, frq, fq_ss, fq_rs)

    @pl.loop(0, 8)
    def _(j):
        me = jnp.logical_and(s == d, j == d)

        @pl.when(jnp.logical_not(me))
        def _():
            remote(fsv.at[j], frv.at[j], fv_ss.at[j], fv_rs.at[j], (g, j, s)).wait_recv()
            remote(fsq.at[j], frq.at[j], fq_ss.at[j], fq_rs.at[j], (g, j, s)).wait_recv()

    for j in range(8):
        lanes = slice(j * 128, j * 128 + 128)
        out_ref[:, lanes] = frq[j, 0:OUT_ROWS, 0:128]
        out_ref[:, INNER + j * 128 : INNER + j * 128 + 128] = frq[j, 0:OUT_ROWS, 128:256]
        out_ref[:, 2 * INNER + j * 128 : 2 * INNER + j * 128 + 128] = frv[j, 0:OUT_ROWS, :]

    for copy in own_sends:
        copy.wait_send()

    @pl.loop(6, 14)
    def _(sem):
        pass_on(0, 0, sem, z_up).wait_send()

    @pl.loop(1, 8)
    def _(j):
        att_copy(lax.rem(s + j, NS)).wait_send()
        ag_copy(j).wait_send()

    @pl.loop(0, 8)
    def _(j):
        ig_copy(j).wait_send()
        norm_copy(j).wait_send()

    @pl.loop(0, 4)
    def _(j):
        qkv_copy(j, 0).wait_send()
        r_copy(j, 0).wait_send()

    @pl.loop(0, S // KB)
    def _(c):
        v_copy(c).wait_send()

    @pl.loop(1, 16)
    def _(j):
        latent_copy(j).wait_send()


    @pl.loop(0, 8)
    def _(c):
        @pl.when(c != d)
        def _():
            dpv_copy(c).wait_send()
            dpq_copy(c).wait_send()

        me = jnp.logical_and(s == d, c == d)

        @pl.when(jnp.logical_not(me))
        def _():
            remote(fsv.at[c], frv.at[s], fv_ss.at[c], fv_rs.at[s], (g, d, c)).wait_send()
            remote(fsq.at[c], frq.at[s], fq_ss.at[c], fq_rs.at[s], (g, d, c)).wait_send()


def scratch_shapes():
    V = pltpu.VMEM
    dma = pltpu.SemaphoreType.DMA
    return [
        V((512, C), BF16),
        V((432, C), BF16),
        V((TOK, D), BF16),
        V((64, TOK), F32),
        V((D, 2 * W3), BF16),
        V((D, INNER), BF16),
        V((64, D), BF16),
        V((NS, TOK, D), BF16),
        V((D, S), BF16),
        V((2 * W3, D), BF16),
        V((4, W3, TOK), BF16),
        V((W3, S), BF16),
        V((4, 8, TOK), F32),
        V((NS, 8, TOK), F32),
        V((512, W3), F32),
        V((16, 32, 128), F32),
        V((16, 32, 128), F32),
        V((512, 128), F32),
        V((TOK, 128), F32),
        V((S, 128), BF16),
        V((2, S, 128), BF16),
        V((2, S, 128), BF16),
        V((2, S, S), F32),
        V((128, S), F32),
        V((128, S), BF16),
        V((S, 128), BF16),
        V((TOK, INNER), BF16),
        V((TOK, D), F32),
        V((TOK, D), F32),
        V((TOK, 128), F32),
        V((TOK, D), BF16),
        V((TOK, INNER), BF16),
        V((S, 128), BF16),
        V((128, S), BF16),
        V((128, S), F32),
        V((S, 128), F32),
        V((S, 256), BF16),
        V((S, 256), BF16),
        V((S, 128), BF16),
        V((S, 128), BF16),
        V((HALF, S), BF16),
        V((2, S), F32),
        V((8, PART, 128), F32),
        V((8, 128, 256), BF16),
        V((8, PART, 128), F32),
        V((8, 128, 256), BF16),
        V((128, 128), F32),
        V((128, 256), F32),
        V((8, 16, 128), F32),
        V((8, 16, 256), F32),
        V((8, 16, 128), F32),
        V((8, 16, 256), F32),
        dma((6,)),
        dma((14,)),
        dma((16,)),
        dma((16,)),
        dma((16,)),
        dma((8,)),
        dma((8,)),
        dma((8,)),
        dma((8,)),
        dma((8,)),
        dma((8,)),
        dma((4,)),
        dma((4,)),
        dma((8,)),
        dma((8,)),
        dma((8,)),
        dma((8,)),
        dma((8,)),
        dma((8,)),
        dma((8,)),
        dma((8,)),
        dma((8,)),
        dma((8,)),
        dma((6,)),
        dma((8,)),
        dma((8,)),
        dma((8,)),
        dma((8,)),
    ]


def local(
    features,
    group_gain,
    group_bias,
    conv_weight,
    hidden,
    modulation,
    timesteps,
    fresh_noise,
    input_weight,
    query_gain,
    key_gain,
    output_weight,
    patch_weight,
):
    vmem = pl.BlockSpec(memory_space=pltpu.VMEM)
    hbm = pl.BlockSpec(memory_space=pl.ANY)
    return pl.pallas_call(
        kernel,
        out_shape=jax.ShapeDtypeStruct((OUT_ROWS, 3 * INNER), F32),
        in_specs=[pl.BlockSpec(memory_space=pltpu.SMEM)] + [vmem] * 5 + [hbm] * 7,
        out_specs=vmem,
        scratch_shapes=scratch_shapes(),
        compiler_params=pltpu.CompilerParams(
            collective_id=0, has_side_effects=True, vmem_limit_bytes=60 * 2**20
        ),
    )(
        timesteps.reshape(1),
        group_gain.reshape(1, C),
        group_bias.reshape(1, C),
        modulation.reshape(3, 1, D),
        query_gain.reshape(1, 64),
        key_gain.reshape(1, 64),
        features.reshape(512, C),
        conv_weight.T,
        hidden.reshape(TOK, D),
        fresh_noise.reshape(TOK, 64).T,
        input_weight,
        output_weight,
        patch_weight.T,
    )


def solution(mesh):
    in_specs = (
        P("dp", None, None, ("grp", "seq"), None, None),
        P(),
        P(),
        P(),
        P("grp", None, "dp", "seq", None),
        P("grp", None, "dp", None, None),
        P("grp", None, "dp"),
        P("grp", None, "dp", "seq", None),
        P(),
        P(),
        P(),
        P(),
        P(),
    )
    out_specs = P(("grp", "seq", "dp"), None)
    return jax.shard_map(local, mesh=mesh, in_specs=in_specs, out_specs=out_specs, check_vma=False)
```

```python
import math

import jax
import jax.numpy as jnp
from jax import lax
from jax.experimental import pallas as pl
from jax.experimental.pallas import tpu as pltpu
from jax.sharding import PartitionSpec as P

F32 = jnp.float32
BF16 = jnp.bfloat16
MESH = pl.DeviceIdType.MESH

NG, NS, ND = 2, 8, 8
D = 1920
INNER = 1024
S = 1024
TOK = 128
W3 = 384
C = 512
HALF = D // NG
PART = HALF // ND
OUT_ROWS = 15
KB = 256
LATENT_SCALE = 1.15258426
GROUP_EPS = 1e-06
LAYER_EPS = 1e-05
HEAD_EPS = 1e-06


def mm(a, b):
    return lax.dot_general(a, b, (((1,), (0,)), ((), ())), preferred_element_type=F32)


def mm_nt(a, b):
    return lax.dot_general(a, b, (((1,), (1,)), ((), ())), preferred_element_type=F32)


def norm_rows(x):
    mu = jnp.mean(x, axis=-1, keepdims=True)
    centred = x - mu
    var = jnp.mean(centred * centred, axis=-1, keepdims=True)
    r = lax.rsqrt(var + LAYER_EPS)
    return centred * r, r


def head_norm_t(x):
    x3 = x.reshape(2, 64, x.shape[1])
    mu = jnp.mean(x3, axis=1, keepdims=True)
    centred = x3 - mu
    var = jnp.mean(centred * centred, axis=1, keepdims=True)
    r = lax.rsqrt(var + HEAD_EPS)
    return (centred * r).reshape(x.shape), r[:, 0, :]


def head_norm_back_t(grad, xhat, r):
    g3 = grad.reshape(2, 64, grad.shape[1])
    x3 = xhat.reshape(2, 64, grad.shape[1])
    mean_g = jnp.mean(g3, axis=1, keepdims=True)
    mean_gx = jnp.mean(g3 * x3, axis=1, keepdims=True)
    return ((g3 - mean_g - x3 * mean_gx) * r[:, None, :]).reshape(grad.shape)


def gain_columns(gain_row):
    both = jnp.concatenate([gain_row, gain_row], axis=1)
    return jnp.broadcast_to(both, (128, 128)).T


def group_mean(v, count):
    lane = lax.broadcasted_iota(jnp.int32, v.shape, 1)
    for step in (1, 2, 4, 8):
        up = pltpu.roll(v, C - step, 1)
        down = pltpu.roll(v, step, 1)
        v = v + jnp.where((lane & step) == 0, up, down)
    return v * (1.0 / count)


def kernel(
    steps,
    ggain,
    gbias,
    mod,
    qgain,
    kgain,
    feat_hbm,
    cw_hbm,
    hid_hbm,
    noise_hbm,
    w_hbm,
    wo_hbm,
    wp_hbm,
    out_ref,
    feat,
    cw,
    hid,
    noise,
    wq,
    wo,
    wp,
    ng,
    nT,
    qkv_send,
    qkvT,
    r_send,
    r_all,
    taps,
    vsend,
    vrecv,
    lat,
    ltok,
    qrow,
    kmask,
    vmask,
    eT,
    num,
    attT,
    att_row,
    att_tok,
    big,
    fin,
    rstd,
    tokbf,
    ag_tok,
    ag_head,
    agT,
    dqT,
    dk,
    ig,
    ig_sib,
    igv,
    igv_sib,
    nT_sib,
    invs,
    wgv,
    wgq,
    dpv,
    dpq,
    accv,
    accq,
    fsv,
    fsq,
    frv,
    frq,
    ld_sem,
    ag_ss,
    ag_rs,
    lt_ss,
    lt_rs,
    a1_ss,
    a1_rs,
    a2_ss,
    a2_rs,
    sb_ss,
    sb_rs,
    sv_ss,
    sv_rs,
    dv_ss,
    dv_rs,
    dq_ss,
    dq_rs,
    fv_ss,
    fv_rs,
    fq_ss,
    fq_rs,
    nt_ss,
    nt_rs,
    w_sem,
    q_ss,
    q_rs,
    r_ss,
    r_rs,
):
    g = lax.axis_index("grp")
    s = lax.axis_index("seq")
    d = lax.axis_index("dp")
    tile = g * NS + s

    def remote(src, dst, ssem, rsem, dev):
        return pltpu.make_async_remote_copy(
            src_ref=src, dst_ref=dst, send_sem=ssem, recv_sem=rsem, device_id=dev, device_id_type=MESH
        )

    def cols(index, width=128):
        return pl.ds(pl.multiple_of(index * width, width), width)

    yh, z = s // 4, lax.rem(s, 4)
    over = (1 - yh) * 4
    across = over + z
    w_loads = [
        pltpu.make_async_copy(
            w_hbm.at[:, cols(owner + 8 * part)],
            wq.at[:, who * W3 + part * 128 : who * W3 + part * 128 + 128],
            w_sem.at[who * 3 + part],
        )
        for who, owner in enumerate((s, across))
        for part in range(3)
    ]
    hid_load = pltpu.make_async_copy(hid_hbm, hid, ld_sem.at[0])
    hid_load.start()
    for copy in w_loads:
        copy.start()

    loads = [
        hid_load,
        pltpu.make_async_copy(feat_hbm, feat, ld_sem.at[1]),
        pltpu.make_async_copy(cw_hbm, cw, ld_sem.at[2]),
        pltpu.make_async_copy(noise_hbm, noise, ld_sem.at[3]),
        pltpu.make_async_copy(wo_hbm, wo, ld_sem.at[4]),
        pltpu.make_async_copy(wp_hbm, wp, ld_sem.at[5]),
    ]
    for copy in loads[1:]:
        copy.start()

    barrier = pltpu.get_barrier_semaphore()

    def greet(dev):
        pl.semaphore_signal(barrier, inc=1, device_id=dev, device_id_type=MESH)

    @pl.loop(1, 16)
    def _(j):
        t = lax.rem(tile + j, 16)
        greet((t // NS, lax.rem(t, NS), d))

    @pl.loop(1, 8)
    def _(j):
        greet((g, s, lax.rem(d + j, ND)))

    @pl.loop(0, 8)
    def _(j):
        me = jnp.logical_and(s == d, j == d)

        @pl.when(jnp.logical_not(me))
        def _():
            greet((g, d, j))
            greet((g, j, s))

    loads[0].wait()
    shift_row = mod[0]
    scale_row = 1.0 + mod[1]

    @pl.loop(0, TOK // 16, unroll=8)
    def _(i):
        rows = pl.ds(pl.multiple_of(i * 16, 16), 16)
        y, _ = norm_rows(hid[rows, :].astype(F32))
        ng[s, rows, :] = (y * scale_row + shift_row).astype(BF16)

    selfs = jnp.where(s == d, 2, 0)
    pl.semaphore_wait(barrier, 15 + 7 + 16 - selfs)

    z_up = yh * 4 + lax.rem(z + 1, 4)
    z_down = yh * 4 + lax.rem(z + 3, 4)

    def pass_on(slot, half, sem, peer):
        block = ng.at[slot, pl.ds(half * 64, 64), :]
        return remote(block, block, ag_ss.at[sem], ag_rs.at[slot * 2 + half], (g, peer, d))

    def arrived(slot, half):
        pass_on(slot, half, 0, z_up).wait_recv()

    z_two = yh * 4 + lax.rem(z + 2, 4)
    over_up = over + lax.rem(z + 1, 4)
    over_down = over + lax.rem(z + 3, 4)
    over_two = over + lax.rem(z + 2, 4)
    own_sends = [
        pass_on(s, 0, 0, z_up),
        pass_on(s, 1, 1, z_down),
        pass_on(s, 0, 2, across),
        pass_on(s, 1, 3, z_up),
        pass_on(s, 0, 4, z_down),
        pass_on(s, 1, 5, across),
    ]
    for copy in own_sends:
        copy.start()

    loads[1].wait()
    loads[2].wait()
    row_id = lax.broadcasted_iota(jnp.int32, (W3, 432), 1)
    col_id = lax.broadcasted_iota(jnp.int32, (W3, 432), 0)
    inner = col_id & 127
    src0 = (col_id >> 7) * 144 + (inner >> 4) * 48 + (inner & 15)
    used = inner < 48
    cw_val = cw[...]
    col_w = lax.broadcasted_iota(jnp.int32, (C, C), 0) & 15
    acts = []
    for clip in range(2):
        x = feat[clip * 256 : clip * 256 + 256, :].astype(F32)
        mean = group_mean(jnp.broadcast_to(jnp.sum(x, axis=0, keepdims=True), (8, C)), 4096.0)[0:1]
        centred = x - mean
        var = group_mean(
            jnp.broadcast_to(jnp.sum(centred * centred, axis=0, keepdims=True), (8, C)), 4096.0
        )[0:1]
        normed = centred * lax.rsqrt(var + GROUP_EPS) * ggain[...] + gbias[...]
        acts.append(normed / (1.0 + jnp.exp(-normed)))
    act = jnp.concatenate(acts, axis=0)
    for e in range(3):
        pick = jnp.where(jnp.logical_and(used, row_id == src0 + e * 16), 1.0, 0.0).astype(BF16)
        we = mm(pick, cw_val).astype(BF16)
        if e == 0:
            ae = jnp.where(col_w == 0, 0.0, pltpu.roll(act, 1, 0))
        elif e == 2:
            ae = jnp.where(col_w == 15, 0.0, pltpu.roll(act, C - 1, 0))
        else:
            ae = act
        term = mm_nt(ae.astype(BF16), we)
        if e == 0:
            taps[...] = term
        else:
            taps[...] += term
    for clip in range(2):
        for frame in range(8):
            total = None
            for a in range(3):
                base = (clip * 8 + max(frame + a - 2, 0)) * 32
                piece = taps[base : base + 32, a * 128 : a * 128 + 128]
                total = piece if total is None else total + piece
            vsend[clip * 8 + frame] = total
    vrecv[tile] = vsend[tile]

    def latent_copy(j):
        t = lax.rem(tile + j, 16)
        return remote(
            vsend.at[t], vrecv.at[tile], lt_ss.at[j], lt_rs.at[tile], (t // NS, lax.rem(t, NS), d)
        )

    def norm_copy(slot):
        return remote(
            nT.at[pl.ds(pl.multiple_of((1 - g) * HALF, 16), HALF), cols(slot)],
            nT_sib.at[:, cols(slot)],
            nt_ss.at[slot],
            nt_rs.at[slot],
            (1 - g, s, d),
        )

    def take(slot):
        nT[:, cols(slot)] = ng[slot].T
        norm_copy(slot).start()

    for copy in w_loads:
        copy.wait()

    gq = gain_columns(qgain[...])
    gk = gain_columns(kgain[...])
    low = lax.broadcasted_iota(jnp.int32, (128, 128), 1) < 64
    r_send[...] = jnp.zeros_like(r_send)

    def hop(j):
        step = jnp.where(j == 1, 3, jnp.where(j == 2, 1, jnp.where(j == 3, 2, 0)))
        return lax.rem(z + step, 4)

    def qkv_copy(j, src):
        return remote(
            qkv_send.at[j], qkvT.at[:, cols(src)], q_ss.at[j], q_rs.at[src], (g, across, d)
        )

    def r_copy(j, src):
        return remote(r_send.at[j], r_all.at[src], r_ss.at[j], r_rs.at[src], (g, across, d))

    def rows_of(here, query, key, value):
        qrow[here, :] = query.T.astype(BF16)
        row = key.T
        kmask[0, here, :] = jnp.where(low, row, 0.0).astype(BF16)
        kmask[1, here, :] = jnp.where(low, 0.0, row).astype(BF16)
        row = value.T
        vmask[0, here, :] = jnp.where(low, row, 0.0).astype(BF16)
        vmask[1, here, :] = jnp.where(low, 0.0, row).astype(BF16)

    @pl.loop(0, 4)
    def _(j):
        src = yh * 4 + hop(j)

        @pl.when(j == 1)
        def _():
            arrived(z_down, 0)
            pass_on(z_down, 0, 6, z_up).start()
            arrived(z_up, 1)
            pass_on(z_up, 1, 7, z_down).start()
            arrived(z_down, 1)

        @pl.when(j == 2)
        def _():
            arrived(z_up, 0)
            for half in range(2):
                arrived(across, half)
                pass_on(across, half, 8 + 2 * half, z_up).start()
                pass_on(across, half, 9 + 2 * half, z_down).start()

        @pl.when(j == 3)
        def _():
            arrived(z_two, 0)
            arrived(z_two, 1)

        here = cols(src)
        for who in (1, 0):
            wide = mm(ng[src], wq[:, who * W3 : who * W3 + W3])
            query, rq = head_norm_t(wide[:, 0:128].T)
            key, rk = head_norm_t(wide[:, 128:256].T)
            query = query * gq
            key = key * gk
            value = wide[:, 256:384].T
            if who == 1:
                qkv_send[j, 0:128, :] = query.astype(BF16)
                qkv_send[j, 128:256, :] = key.astype(BF16)
                qkv_send[j, 256:384, :] = value.astype(BF16)
                r_send[j, 0:2, :] = rq
                r_send[j, 2:4, :] = rk
                qkv_copy(j, src).start()
                r_copy(j, src).start()
            else:
                qkvT[0:128, here] = query.astype(BF16)
                qkvT[128:256, here] = key.astype(BF16)
                qkvT[256:384, here] = value.astype(BF16)
                r_all[src] = jnp.zeros((8, TOK), F32)
                r_all[src, 0:2, :] = rq
                r_all[src, 2:4, :] = rk
                rows_of(here, query, key, value)
        take(src)

    @pl.loop(1, 16)
    def _(j):
        latent_copy(j).start()

    @pl.loop(0, 4)
    def _(j):
        src = over + hop(j)
        qkv_copy(j, src).wait_recv()
        r_copy(j, src).wait_recv()
        here = cols(src)
        rows_of(
            here,
            qkvT[0:128, here].astype(F32),
            qkvT[128:256, here].astype(F32),
            qkvT[256:384, here].astype(F32),
        )

    qT = qkvT.at[0:128]
    kT = qkvT.at[128:256]
    vT = qkvT.at[256:384]

    def att_copy(peer):
        return remote(
            att_row.at[cols(peer), :],
            att_tok.at[:, cols(s)],
            a1_ss.at[peer],
            a1_rs.at[s],
            (g, peer, d),
        )

    @pl.loop(0, S // KB)
    def _(j):
        c = lax.rem(s // 2 + 1 + j, S // KB)
        here = cols(c, KB)
        for h in range(2):
            hr = slice(h * 64, h * 64 + 64)
            e = jnp.exp(mm(kmask[h], qT[:, here]) * 0.125)
            eT[h, :, here] = e
            inv = 1.0 / jnp.sum(e, axis=0, keepdims=True)
            invs[h : h + 1, here] = inv
            num[hr, here] = mm(vT[hr, :], e.astype(BF16)) * inv
        val = num[:, here]
        attT[:, here] = val.astype(BF16)
        att_row[here, :] = val.T.astype(BF16)
        for q in range(2):
            peer = 2 * c + q

            @pl.when(peer != s)
            def _():
                att_copy(peer).start()

    att_tok[:, cols(s)] = att_row[cols(s), :]

    arrived(over_down, 0)
    pass_on(over_down, 0, 12, z_up).start()
    arrived(over_up, 1)
    pass_on(over_up, 1, 13, z_down).start()

    @pl.loop(1, 16)
    def _(j):
        t = lax.rem(tile + j, 16)
        remote(
            vsend.at[t], vrecv.at[t], lt_ss.at[j], lt_rs.at[t], (t // NS, lax.rem(t, NS), d)
        ).wait_recv()

    x = vrecv[...].reshape(512, 128)
    pad = jnp.zeros((16, 128), F32)
    total = jnp.concatenate([pad, x[:-16]], axis=0) + pltpu.roll(x, 112, 1)
    total = total + jnp.concatenate([pltpu.roll(x, 96, 1)[16:], pad], axis=0)
    lane = lax.broadcasted_iota(jnp.int32, (512, 128), 1)
    lat[...] = jnp.where(lane < 16, total * LATENT_SCALE, 0.0)
    tokens = jnp.zeros((128, 128), F32)
    for jj in range(2):
        half = lat[pl.ds(jj, 256, stride=2), :].reshape(16, 2, 8, 128)
        for ii in range(2):
            piece = half[:, ii].reshape(128, 128)
            place = 16 * (2 * ii + jj)
            tokens = tokens + (pltpu.roll(piece, place, 1) if place else piece)
    ltok[...] = tokens

    arrived(over_down, 1)
    arrived(over_up, 0)

    @pl.loop(0, 3)
    def _(j):
        take(jnp.where(j == 0, across, jnp.where(j == 1, over_down, over_up)))

    for index in (3, 4, 5):
        loads[index].wait()

    @pl.loop(1, 8)
    def _(j):
        src = lax.rem(s + 8 - j, NS)
        remote(
            att_row.at[cols(src), :], att_tok.at[:, cols(src)], a1_ss.at[src], a1_rs.at[src], (g, src, d)
        ).wait_recv()

    big[...] = mm_nt(att_tok[...], wo[...])
    gate_row = mod[2]

    @pl.loop(0, TOK // 16, unroll=8)
    def _(i):
        rows = pl.ds(pl.multiple_of(i * 16, 16), 16)
        mixed = hid[rows, :].astype(F32) + gate_row * big[rows, :]
        y, r = norm_rows(mixed)
        fin[rows, :] = y
        rstd[rows, :] = jnp.broadcast_to(r, (16, 128))
        tokbf[rows, :] = y.astype(BF16)

    step = jnp.full((TOK, 64), steps[0], jnp.int32).astype(F32)
    angle = (step / 1000 + 0.008) / 1.008 * (math.pi / 2)
    target = jnp.cos(angle) * noise[...].T - jnp.sin(angle) * ltok[:, 0:64]
    pred_grad = ((2.0 / 64) * (mm_nt(tokbf[...], wp[...]) - target)).astype(BF16)
    big[...] = mm(pred_grad, wp[...])

    @pl.loop(0, TOK // 16, unroll=8)
    def _(i):
        rows = pl.ds(pl.multiple_of(i * 16, 16), 16)
        dy = big[rows, :]
        y = fin[rows, :]
        mean_dy = jnp.mean(dy, axis=-1, keepdims=True)
        mean_dyy = jnp.mean(dy * y, axis=-1, keepdims=True)
        dx = (dy - mean_dy - y * mean_dyy) * rstd[rows, 0:1]
        tokbf[rows, :] = (gate_row * dx).astype(BF16)

    def ag_copy(peer):
        return remote(
            ag_tok.at[:, cols(peer)], ag_head.at[cols(s), :], a2_ss.at[peer], a2_rs.at[s], (g, peer, d)
        )

    @pl.loop(0, 4)
    def _(j):
        c = lax.rem(s // 2 + 1 + j, 4)
        ag_tok[:, cols(c, 256)] = mm(tokbf[...], wo[:, cols(c, 256)]).astype(BF16)
        for q in range(2):
            peer = 2 * c + q

            @pl.when(peer != s)
            def _():
                ag_copy(peer).start()

    ag_head[cols(s), :] = ag_tok[:, cols(s)]
    @pl.loop(1, 8)
    def _(j):
        src = lax.rem(s + 8 - j, NS)
        remote(
            ag_tok.at[:, cols(src)], ag_head.at[cols(src), :], a2_ss.at[src], a2_rs.at[src], (g, src, d)
        ).wait_recv()

    @pl.loop(0, 8)
    def _(j):
        here = cols(j)
        val = ag_head[here, :].astype(F32).T
        agT[:, here] = val.astype(BF16)
        num[:, here] = val * attT[:, here].astype(F32)

    def v_copy(c):
        rows = cols(c, KB)
        return remote(
            igv.at[rows, :], igv_sib.at[rows, :], sv_ss.at[c], sv_rs.at[c], (1 - g, s, d)
        )

    low_k = lax.broadcasted_iota(jnp.int32, (KB, 128), 1) < 64

    @pl.loop(0, S // KB)
    def _(c):
        rows = cols(c, KB)
        dvs = []
        for h in range(2):
            p = eT[h, rows, :] * invs[h : h + 1, :]
            dvs.append(mm(p.astype(BF16), ag_head[...]))
        igv[rows, :] = jnp.where(low_k, dvs[0], dvs[1]).astype(BF16)
        v_copy(c).start()

    deltas = [jnp.sum(num[h * 64 : h * 64 + 64, :], axis=0, keepdims=True) for h in range(2)]
    dqT[...] = jnp.zeros_like(dqT)

    def score_back(c):
        rows = cols(c, KB)
        dks = []
        for h in range(2):
            p = eT[h, rows, :] * invs[h : h + 1, :]
            dp = mm(vmask[h, rows, :], agT[...])
            ds = (p * (dp - deltas[h])).astype(BF16)
            dks.append(mm(ds, qrow[...]))
            hr = slice(h * 64, h * 64 + 64)
            dqT[hr, :] += mm(kT[hr, rows], ds)
        dk[rows, :] = jnp.where(low_k, dks[0], dks[1]) * 0.125

    @pl.loop(0, 2)
    def _(c):
        score_back(c)

    def grad_rows(j, i, mine, theirs, wait_theirs):
        rows = pl.ds(pl.multiple_of(g * HALF + i * 240, 16), 240)
        value = mm(nT[rows, :], mine[...])

        @pl.when(j == 0)
        def _():
            wait_theirs()

        return value + mm(nT_sib[pl.ds(pl.multiple_of(i * 240, 16), 240), :], theirs[...])

    def padded(value, q):
        blank = jnp.zeros((128 - PART, value.shape[1]), F32)
        return jnp.concatenate([value[q * PART : q * PART + PART], blank], axis=0)

    def dpv_copy(c):
        return remote(wgv.at[c], dpv.at[d], dv_ss.at[c], dv_rs.at[d], (g, s, c))

    def dpq_copy(c):
        return remote(wgq.at[c], dpq.at[d], dq_ss.at[c], dq_rs.at[d], (g, s, c))

    arrived(over_two, 0)
    arrived(over_two, 1)

    take(over_two)

    def wait_v():
        @pl.loop(0, 8)
        def _(j):
            norm_copy(j).wait_recv()

        @pl.loop(0, S // KB)
        def _(c):
            v_copy(c).wait_recv()

    def wait_ig():
        @pl.loop(0, 8)
        def _(j):
            ig_copy(j).wait_recv()

    @pl.loop(0, 4)
    def _(j):
        i = lax.rem(d // 2 + 1 + j, 4)
        value = grad_rows(j, i, igv, igv_sib, wait_v)
        for q in range(2):
            c = 2 * i + q
            part = padded(value, q)

            @pl.when(c == d)
            def _():
                accv[...] = part

            @pl.when(c != d)
            def _():
                wgv[c] = part[0:PART]
                dpv_copy(c).start()

    @pl.loop(2, 4)
    def _(c):
        score_back(c)

    inv_gq = 1.0 / gq
    inv_gk = 1.0 / gk

    def ig_copy(j):
        here = cols(j)
        return remote(
            ig.at[here, :], ig_sib.at[here, :], sb_ss.at[j], sb_rs.at[j], (1 - g, s, d)
        )

    @pl.loop(0, 8)
    def _(j):
        here = cols(j)
        xhat = qT[:, here].astype(F32) * inv_gq
        grad = head_norm_back_t(dqT[:, here] * 0.125 * gq, xhat, r_all[j, 0:2, :])
        ig[here, 0:128] = grad.T.astype(BF16)
        xhat = kT[:, here].astype(F32) * inv_gk
        grad = head_norm_back_t(dk[here, :].T * gk, xhat, r_all[j, 2:4, :])
        ig[here, 128:256] = grad.T.astype(BF16)
        ig_copy(j).start()

    @pl.loop(0, 4)
    def _(j):
        i = lax.rem(d // 2 + 1 + j, 4)
        value = grad_rows(j, i, ig, ig_sib, wait_ig)
        for q in range(2):
            c = 2 * i + q
            part = padded(value, q)

            @pl.when(c == d)
            def _():
                accq[...] = part

            @pl.when(c != d)
            def _():
                wgq[c] = part.astype(BF16)
                dpq_copy(c).start()

    def finish_columns(own, arrived, part_sem, total, out_send, out_recv, send_sem, recv_sem):
        @pl.loop(1, 8)
        def _(j):
            src = lax.rem(d + 8 - j, ND)
            remote(own.at[src], arrived.at[src], part_sem.at[src], part_sem.at[src], (g, s, src)).wait_recv()
            total[0 : arrived.shape[1], :] += arrived[src].astype(F32)

        for j in range(8):
            out_send[j] = total[j * OUT_ROWS : j * OUT_ROWS + 16, :]

        @pl.loop(0, 8)
        def _(j):
            me = jnp.logical_and(s == d, j == d)

            @pl.when(me)
            def _():
                out_recv[s] = out_send[j]

            @pl.when(jnp.logical_not(me))
            def _():
                remote(
                    out_send.at[j], out_recv.at[s], send_sem.at[j], recv_sem.at[s], (g, d, j)
                ).start()

    finish_columns(wgv, dpv, dv_rs, accv, fsv, frv, fv_ss, fv_rs)
    finish_columns(wgq, dpq, dq_rs, accq, fsq, frq, fq_ss, fq_rs)

    @pl.loop(0, 8)
    def _(j):
        me = jnp.logical_and(s == d, j == d)

        @pl.when(jnp.logical_not(me))
        def _():
            remote(fsv.at[j], frv.at[j], fv_ss.at[j], fv_rs.at[j], (g, j, s)).wait_recv()
            remote(fsq.at[j], frq.at[j], fq_ss.at[j], fq_rs.at[j], (g, j, s)).wait_recv()

    for j in range(8):
        lanes = slice(j * 128, j * 128 + 128)
        out_ref[:, lanes] = frq[j, 0:OUT_ROWS, 0:128]
        out_ref[:, INNER + j * 128 : INNER + j * 128 + 128] = frq[j, 0:OUT_ROWS, 128:256]
        out_ref[:, 2 * INNER + j * 128 : 2 * INNER + j * 128 + 128] = frv[j, 0:OUT_ROWS, :]

    for copy in own_sends:
        copy.wait_send()

    @pl.loop(6, 14)
    def _(sem):
        pass_on(0, 0, sem, z_up).wait_send()

    @pl.loop(1, 8)
    def _(j):
        att_copy(lax.rem(s + j, NS)).wait_send()
        ag_copy(lax.rem(s + j, NS)).wait_send()

    @pl.loop(0, 8)
    def _(j):
        ig_copy(j).wait_send()
        norm_copy(j).wait_send()

    @pl.loop(0, 4)
    def _(j):
        qkv_copy(j, 0).wait_send()
        r_copy(j, 0).wait_send()

    @pl.loop(0, S // KB)
    def _(c):
        v_copy(c).wait_send()

    @pl.loop(1, 16)
    def _(j):
        latent_copy(j).wait_send()


    @pl.loop(0, 8)
    def _(c):
        @pl.when(c != d)
        def _():
            dpv_copy(c).wait_send()
            dpq_copy(c).wait_send()

        me = jnp.logical_and(s == d, c == d)

        @pl.when(jnp.logical_not(me))
        def _():
            remote(fsv.at[c], frv.at[s], fv_ss.at[c], fv_rs.at[s], (g, d, c)).wait_send()
            remote(fsq.at[c], frq.at[s], fq_ss.at[c], fq_rs.at[s], (g, d, c)).wait_send()


def scratch_shapes():
    V = pltpu.VMEM
    dma = pltpu.SemaphoreType.DMA
    return [
        V((512, C), BF16),
        V((432, C), BF16),
        V((TOK, D), BF16),
        V((64, TOK), F32),
        V((D, 2 * W3), BF16),
        V((D, INNER), BF16),
        V((64, D), BF16),
        V((NS, TOK, D), BF16),
        V((D, S), BF16),
        V((4, W3, TOK), BF16),
        V((W3, S), BF16),
        V((4, 8, TOK), F32),
        V((NS, 8, TOK), F32),
        V((512, W3), F32),
        V((16, 32, 128), F32),
        V((16, 32, 128), F32),
        V((512, 128), F32),
        V((TOK, 128), F32),
        V((S, 128), BF16),
        V((2, S, 128), BF16),
        V((2, S, 128), BF16),
        V((2, S, S), F32),
        V((128, S), F32),
        V((128, S), BF16),
        V((S, 128), BF16),
        V((TOK, INNER), BF16),
        V((TOK, D), F32),
        V((TOK, D), F32),
        V((TOK, 128), F32),
        V((TOK, D), BF16),
        V((TOK, INNER), BF16),
        V((S, 128), BF16),
        V((128, S), BF16),
        V((128, S), F32),
        V((S, 128), F32),
        V((S, 256), BF16),
        V((S, 256), BF16),
        V((S, 128), BF16),
        V((S, 128), BF16),
        V((HALF, S), BF16),
        V((2, S), F32),
        V((8, PART, 128), F32),
        V((8, 128, 256), BF16),
        V((8, PART, 128), F32),
        V((8, 128, 256), BF16),
        V((128, 128), F32),
        V((128, 256), F32),
        V((8, 16, 128), F32),
        V((8, 16, 256), F32),
        V((8, 16, 128), F32),
        V((8, 16, 256), F32),
        dma((6,)),
        dma((14,)),
        dma((16,)),
        dma((16,)),
        dma((16,)),
        dma((8,)),
        dma((8,)),
        dma((8,)),
        dma((8,)),
        dma((8,)),
        dma((8,)),
        dma((4,)),
        dma((4,)),
        dma((8,)),
        dma((8,)),
        dma((8,)),
        dma((8,)),
        dma((8,)),
        dma((8,)),
        dma((8,)),
        dma((8,)),
        dma((8,)),
        dma((8,)),
        dma((6,)),
        dma((8,)),
        dma((8,)),
        dma((8,)),
        dma((8,)),
    ]


def local(
    features,
    group_gain,
    group_bias,
    conv_weight,
    hidden,
    modulation,
    timesteps,
    fresh_noise,
    input_weight,
    query_gain,
    key_gain,
    output_weight,
    patch_weight,
):
    vmem = pl.BlockSpec(memory_space=pltpu.VMEM)
    hbm = pl.BlockSpec(memory_space=pl.ANY)
    return pl.pallas_call(
        kernel,
        out_shape=jax.ShapeDtypeStruct((OUT_ROWS, 3 * INNER), F32),
        in_specs=[pl.BlockSpec(memory_space=pltpu.SMEM)] + [vmem] * 5 + [hbm] * 7,
        out_specs=vmem,
        scratch_shapes=scratch_shapes(),
        compiler_params=pltpu.CompilerParams(
            collective_id=0, has_side_effects=True, vmem_limit_bytes=60 * 2**20
        ),
    )(
        timesteps.reshape(1),
        group_gain.reshape(1, C),
        group_bias.reshape(1, C),
        modulation.reshape(3, 1, D),
        query_gain.reshape(1, 64),
        key_gain.reshape(1, 64),
        features.reshape(512, C),
        conv_weight.T,
        hidden.reshape(TOK, D),
        fresh_noise.reshape(TOK, 64).T,
        input_weight,
        output_weight,
        patch_weight.T,
    )


def solution(mesh):
    in_specs = (
        P("dp", None, None, ("grp", "seq"), None, None),
        P(),
        P(),
        P(),
        P("grp", None, "dp", "seq", None),
        P("grp", None, "dp", None, None),
        P("grp", None, "dp"),
        P("grp", None, "dp", "seq", None),
        P(),
        P(),
        P(),
        P(),
        P(),
    )
    out_specs = P(("grp", "seq", "dp"), None)
    return jax.shard_map(local, mesh=mesh, in_specs=in_specs, out_specs=out_specs, check_vma=False)
```
